32 devices in a mesh: pipe: 2 (over y), expert: 16 (over z, x, core).
Axes of the slice: x: 2, y: 2, z: 4, core: 2. Of those that a mesh axis runs over, the one named last changes fastest.
Arguments:
- tokens: bfloat16 [4096, 2048], P(('pipe', 'expert')), may hold values from -6 to 6
- cotangent: bfloat16 [4096, 2048], P(('pipe', 'expert')), may hold values from -6 to 6
- expert_ids: int32 [4096, 8], P(('pipe', 'expert')), may hold values from 0 to 127, all different within a row
- gates: float32 [4096, 8], P(('pipe', 'expert')), may hold values from 0.05 to 0.5
- w_gate: bfloat16 [2, 2048, 3072], P('pipe', None, 'expert'), as said below
- w_up: bfloat16 [2, 2048, 3072], P('pipe', None, 'expert'), as said below
- w_down: bfloat16 [2, 3072, 2048], P('pipe', 'expert'), as said below
Outputs:
- mixed_out: bfloat16 [4096, 2048], P(('pipe', 'expert'))
- token_grad: bfloat16 [4096, 2048], P(('pipe', 'expert'))
- gate_grad: float32 [4096, 8], P(('pipe', 'expert'))
- down_grad: bfloat16 [2, 3072, 1024], P('pipe', 'expert')
The draws below stay inside these ranges and needn't reach their ends.
Inputs may be any that keep to these rules, and one draw needn't show every extreme that they name: `expert_ids`: each row names 8 different experts. `w_gate`: the blocks of pipe index p and 1 - p are equal. `w_up`: the blocks of pipe index p and 1 - p are equal. `w_down`: the blocks of pipe index p and 1 - p are equal.
All inputs are finite; a program needn't handle non-finite values.
Results may differ from the reference program's by a relative error of at most 0.0065.
Values may be sent and summed in bfloat16 or wider, within the bound.
A program may use at most 64 MiB of HBM per device.

```python
import math
import jax
import jax.numpy as jnp
from jax import lax

D = 2048
EXPERTS = 128
TOPK = 8
FFW = 768
WS = 4
FS = 192
EW = 4
TOK_DEV = 128
CAP = 5
TOKENS = 4096
N_PIPE = 2
N_EXPERT = 16


def mirrored(key, rows, cols, fan_in):
    half_set = jnp.clip(jax.random.normal(key, (N_PIPE // 2, rows, cols), jnp.float32), -6.0, 6.0) * fan_in ** (-0.5)
    return jnp.concatenate([half_set, half_set[::-1]], axis=0)


def draw_w_gate(key, part):
    return mirrored(jax.random.fold_in(key, 101), D, EW * FFW, D).astype(jnp.bfloat16)


def draw_w_up(key, part):
    return mirrored(jax.random.fold_in(key, 202), D, EW * FFW, D).astype(jnp.bfloat16)


def draw_w_down(key, part):
    return mirrored(jax.random.fold_in(key, 303), EW * FFW, D, FFW).astype(jnp.bfloat16)


def block_levels(key, shape, split, least, top_value):
    def one(position, shards_of):
        draws = jax.random.uniform(jax.random.fold_in(jax.random.fold_in(key, 6), position), (shards_of,), jnp.float32, least / len(split), top_value / len(split))
        return jnp.repeat(jnp.exp(draws), shape[position] // shards_of).reshape((-1,) + (1,) * (len(shape) - position - 1))

    gain = one(*split[0])
    for cut in split[1:]:
        gain = gain * one(*cut)
    return gain


def picks_of(own_key, rows, count, top, lift):
    sequence = jax.random.permutation(jax.random.fold_in(own_key, 1), count)
    pull = sequence
    for power in range(3):
        pull = pull * pull // count
    pull = pull * lift // count
    tickets = jax.random.randint(jax.random.fold_in(own_key, 2), (rows, count), 0, 4096) + pull
    sure = jax.random.permutation(jax.random.fold_in(own_key, 3), rows)[jnp.arange(count) % rows]
    tickets = jnp.where(jnp.arange(rows)[:, None] == sure[None, :], 1 << 14, tickets)
    score = tickets * count + jnp.arange(count)
    return lax.top_k(score.astype(jnp.int32), top)[1].astype(jnp.int32)


def centred(rng, dims, width, bound, pieces=(), held_as=jnp.bfloat16):
    array = jax.random.normal(rng, dims, jnp.float32) * width
    if len(pieces) > 0:
        array = block_levels(rng, dims, pieces, -0.22, 0.18) * array
    return jnp.clip(array, min=-bound, max=bound).astype(held_as)


def setup_inputs(seed: int = 0) -> dict:
    keys = jax.random.split(jax.random.key(seed), 8)
    tokens = centred(keys[0], (TOKENS, D), 1.0, 6.0, ((0, 32),))
    cotangent = centred(keys[1], (TOKENS, D), 1.0, 6.0, ((0, 32),))
    expert_ids = picks_of(keys[2], TOKENS, EXPERTS, TOPK, 1024)
    gates = jnp.clip(jnp.exp(math.log(0.5) - 2.3025851 * jax.random.uniform(keys[3], (TOKENS, TOPK), jnp.float32) ** block_levels(keys[3], (TOKENS, TOPK), ((0, 32),), -0.2, 0.2)), 0.05, 0.5)
    w_gate = draw_w_gate(jax.random.fold_in(keys[7], 71), 0)
    w_up = draw_w_up(jax.random.fold_in(keys[7], 71), 0)
    w_down = draw_w_down(jax.random.fold_in(keys[7], 71), 0)
    return dict(tokens=tokens, cotangent=cotangent, expert_ids=expert_ids, gates=gates, w_gate=w_gate, w_up=w_up, w_down=w_down)


def silu_parts(preact):
    sigmoid_val = jax.nn.sigmoid(preact)
    return preact * sigmoid_val, sigmoid_val * (1.0 + preact * (1.0 - sigmoid_val))


def rounded_f32(values):
    return lax.optimization_barrier(values.astype(jnp.bfloat16)).astype(jnp.float32)


def section_layer(rows_in, rows_cot, ids_here, gates_here, gate_mat, up_mat, down_mat):
    tok_rows = rows_in.shape[0]
    row_bound = N_EXPERT * CAP
    padded_in = jnp.concatenate([rows_in, jnp.zeros((1, D), rows_in.dtype)])
    padded_cot = jnp.concatenate([rows_cot, jnp.zeros((1, D), rows_cot.dtype)])
    highest = lax.Precision.HIGHEST

    def one_expert(expert_no):
        gate_cols = lax.dynamic_slice_in_dim(gate_mat, expert_no * FFW, FFW, 1)
        up_cols = lax.dynamic_slice_in_dim(up_mat, expert_no * FFW, FFW, 1)
        down_rows = lax.dynamic_slice_in_dim(down_mat, expert_no * FFW, FFW, 0)
        named = (ids_here == expert_no).astype(jnp.int32).reshape(N_EXPERT, TOK_DEV * TOPK)
        before = jnp.cumsum(named, axis=1) - named
        matches = ((named == 1) & (before < CAP)).reshape(tok_rows, TOPK)
        row_gate = jnp.sum(jnp.where(matches, gates_here, 0.0), axis=1)
        gate_padded = jnp.concatenate([row_gate, jnp.zeros((1,), row_gate.dtype)])
        chosen = jnp.nonzero(jnp.any(matches, axis=1), size=row_bound, fill_value=tok_rows)[0].astype(jnp.int32)
        inputs = padded_in[chosen]
        cot_rows = padded_cot[chosen].astype(jnp.float32)
        slot_gate = gate_padded[chosen]
        scaled = (slot_gate[:, None] * cot_rows).astype(jnp.bfloat16)
        gate_pre = jnp.dot(inputs, gate_cols, preferred_element_type=jnp.float32)
        up_pre = jnp.dot(inputs, up_cols, preferred_element_type=jnp.float32)
        activated, slope_val = silu_parts(gate_pre)
        hidden = (activated * up_pre).astype(jnp.bfloat16)
        hidden_groups = hidden.astype(jnp.float32).reshape(row_bound, WS, FS)
        down_groups = down_rows.astype(jnp.float32).reshape(WS, FS, D)
        group_out = jnp.einsum("rgf,gfd->grd", hidden_groups, down_groups, precision=highest)
        expert_out = jnp.sum(rounded_f32(group_out), axis=0)
        hidden_grad = jnp.dot(scaled, down_rows.T, preferred_element_type=jnp.float32)
        grad_gate = (hidden_grad * up_pre * slope_val).astype(jnp.bfloat16)
        grad_up = (hidden_grad * activated).astype(jnp.bfloat16)
        gate_groups = gate_cols.astype(jnp.float32).reshape(D, WS, FS)
        up_groups = up_cols.astype(jnp.float32).reshape(D, WS, FS)
        back_gate = jnp.einsum("rgf,dgf->grd", grad_gate.astype(jnp.float32).reshape(row_bound, WS, FS), gate_groups, precision=highest)
        back_up = jnp.einsum("rgf,dgf->grd", grad_up.astype(jnp.float32).reshape(row_bound, WS, FS), up_groups, precision=highest)
        token_part = jnp.sum(rounded_f32(back_gate + back_up), axis=0)
        down_part = jnp.dot(hidden.T, scaled, preferred_element_type=jnp.float32)
        slot_value = jnp.sum(cot_rows * expert_out, axis=1)
        match_padded = jnp.concatenate([matches, jnp.zeros((1, TOPK), jnp.bool_)])
        gate_part = slot_value[:, None] * match_padded[chosen].astype(jnp.float32)
        return chosen, slot_gate, expert_out, token_part, down_part, gate_part

    chosen, slot_gate, expert_out, token_part, down_part, gate_part = lax.map(one_expert, jnp.arange(EW, dtype=jnp.int32))
    flat_rows = chosen.reshape(-1)
    mixed_sum = jnp.zeros((tok_rows + 1, D), jnp.float32).at[flat_rows].add((slot_gate[:, :, None] * expert_out).reshape(-1, D))
    token_sum = jnp.zeros((tok_rows + 1, D), jnp.float32).at[flat_rows].add(token_part.reshape(-1, D))
    gate_sum = jnp.zeros((tok_rows + 1, TOPK), jnp.float32).at[flat_rows].add(gate_part.reshape(-1, TOPK))
    return (mixed_sum[:tok_rows].astype(jnp.bfloat16), token_sum[:tok_rows].astype(jnp.bfloat16),
            gate_sum[:tok_rows], down_part.reshape(EW * FFW, D))


def reference(tokens, cotangent, expert_ids, gates, w_gate, w_up, w_down):
    per_section = N_EXPERT * TOK_DEV
    mixed_list, token_list, gate_list, local_list = [], [], [], []
    for section_no in range(N_PIPE):
        first_row = section_no * per_section
        results = section_layer(tokens[first_row:first_row + per_section], cotangent[first_row:first_row + per_section],
                              expert_ids[first_row:first_row + per_section], gates[first_row:first_row + per_section],
                              w_gate[section_no], w_up[section_no], w_down[section_no])
        mixed_list.append(results[0])
        token_list.append(results[1])
        gate_list.append(results[2])
        local_list.append(results[3])
    local_down = rounded_f32(jnp.stack(local_list))
    summed = local_down + local_down[::-1]
    half_width = D // 2
    halves = []
    for section_no in range(N_PIPE):
        offset = half_width if section_no >= N_PIPE // 2 else 0
        halves.append(summed[section_no, :, offset:offset + half_width])
    down_grad = jnp.stack(halves).astype(jnp.bfloat16)
    return (jnp.concatenate(mixed_list), jnp.concatenate(token_list), jnp.concatenate(gate_list), down_grad)
```

```python
import functools

import jax
import jax.numpy as jnp
from jax import lax
from jax.experimental import pallas as pl
from jax.experimental.pallas import tpu as pltpu
from jax.sharding import PartitionSpec as P

WS = 4
LANES = 128
BF16 = jnp.bfloat16
F32 = jnp.float32
MESH = pl.DeviceIdType.MESH


def dot(a, b, dims=((1,), (0,))):
    return lax.dot_general(a, b, (dims, ((), ())), preferred_element_type=F32)


def kernel(
    sections,
    devices,
    capacity,
    tokens_hbm,
    cot_hbm,
    ids_ref,
    gates_ref,
    gate_hbm,
    up_hbm,
    down_hbm,
    mixed_ref,
    token_ref,
    gate_grad_ref,
    down_grad_ref,
    tokens,
    cot,
    w_gate,
    w_up,
    w_down,
    wide_a,
    wide_b,
    slot_cot,
    sent,
    held,
    rows_in,
    rows_scaled,
    hidden_own,
    hidden_other,
    scaled_other,
    terms,
    from_core,
    to_x,
    from_x,
    to_owner,
    returned,
    load_sem,
    z_send,
    z_recv,
    f_send,
    f_recv,
    p_send,
    p_recv,
    a_send,
    a_recv,
    b_send,
    b_recv,
    c_send,
    c_recv,
):
    experts = devices // WS
    pieces = tokens.shape[1] // LANES
    tok_count, width = tokens.shape
    half = width // 2
    part = capacity * pieces
    slots = slot_cot.shape[0]
    row_count = devices * capacity
    section = lax.axis_index("pipe")
    me = lax.axis_index("expert")
    w, g = me // WS, me % WS
    x, core = g // 2, g % 2
    mirror = sections - 1 - section
    sibling = w * WS + x * 2 + (1 - core)
    across = w * WS + (1 - x) * 2 + core

    def owner(expert):
        return expert * WS + g

    def remote(src, dst, send, recv, pipe_pos, expert_pos):
        return pltpu.make_async_remote_copy(
            src_ref=src,
            dst_ref=dst,
            send_sem=send,
            recv_sem=recv,
            device_id=(pipe_pos, expert_pos),
            device_id_type=MESH,
        )

    loads = [
        pltpu.make_async_copy(src, dst, load_sem.at[i])
        for i, (src, dst) in enumerate(
            [
                (tokens_hbm, tokens),
                (cot_hbm, cot),
                (gate_hbm.at[0], w_gate),
                (up_hbm.at[0], w_up),
                (down_hbm.at[0], w_down),
            ]
        )
    ]
    for load in loads:
        load.start()
    barrier = pltpu.get_barrier_semaphore()
    for d in range(1, experts):
        pl.semaphore_signal(
            barrier,
            inc=1,
            device_id=(section, owner(lax.rem(w + d, experts))),
            device_id_type=MESH,
        )
    for target in ((section, sibling), (section, across), (mirror, me)):
        pl.semaphore_signal(barrier, inc=1, device_id=target, device_id_type=MESH)

    lane = lax.broadcasted_iota(jnp.int32, (tok_count, LANES), 1)
    lane_expert = jnp.where(lane < experts * capacity, lane // capacity, -1)
    lane_rank = (lane % capacity).astype(F32)
    ids = ids_ref[...]
    gates = gates_ref[...]
    chosen = ids.shape[1]
    named = [ids[:, k : k + 1] == lane_expert for k in range(chosen)]
    match = jnp.zeros((tok_count, LANES), F32)
    weight = jnp.zeros((tok_count, LANES), F32)
    for k in range(chosen):
        match += jnp.where(named[k], 1.0, 0.0)
        weight += jnp.where(named[k], gates[:, k : k + 1], 0.0)
    row_no = lax.broadcasted_iota(jnp.int32, (tok_count, tok_count), 0)
    col_no = lax.broadcasted_iota(jnp.int32, (tok_count, tok_count), 1)
    below = jnp.where(col_no < row_no, 1.0, 0.0).astype(BF16)
    earlier = dot(below, match.astype(BF16))
    pick = jnp.where((match > 0.5) & (earlier == lane_rank), 1.0, 0.0)
    pick_gate = pick * weight
    slot_gate = jnp.sum(pick_gate.T, axis=1, keepdims=True)[:slots]
    pick_rows = pick.T[:slots].astype(BF16)

    def to_wire(scratch, values, count):
        for j in range(pieces):
            scratch[pl.ds(j, count, stride=pieces), :] = values[
                :, j * LANES : (j + 1) * LANES
            ]

    loads[0].wait()
    to_wire(wide_a, dot(pick_rows, tokens[...]), slots)
    loads[1].wait()
    cot_rows = dot(pick_rows, cot[...])
    slot_cot[...] = cot_rows
    to_wire(wide_b, slot_gate * cot_rows, slots)
    for e in range(experts):
        sent[e, :part] = wide_a[e * part : (e + 1) * part].astype(BF16)
        sent[e, part:] = wide_b[e * part : (e + 1) * part].astype(BF16)
    held[w, g] = sent[w]
    pl.semaphore_wait(barrier, experts + 2)

    outgoing = []
    for d in range(experts - 1, 0, -1):
        to = lax.rem(w + d, experts)
        copy = remote(
            sent.at[to], held.at[w, g], z_send.at[d], z_recv.at[d], section, owner(to)
        )
        copy.start()
        outgoing.append(copy)
    g_core = x * 2 + (1 - core)
    g_across = (1 - x) * 2 + core
    g_far = (1 - x) * 2 + (1 - core)
    order = [0] + list(range(1, experts))
    for d in order:
        src = lax.rem(w - d + experts, experts)
        block = held.at[src, g]
        if d:
            remote(
                block, block, z_send.at[d], z_recv.at[d], section, me ^ 1
            ).wait_recv()
        for n, to in enumerate((across, sibling)):
            copy = remote(block, block, f_send.at[n, d], f_recv.at[n, d], section, to)
            copy.start()
            outgoing.append(copy)
    for d in order:
        src = lax.rem(w - d + experts, experts)
        block = held.at[src, g_across]
        remote(
            block, block, f_send.at[0, d], f_recv.at[0, d], section, across
        ).wait_recv()
        copy = remote(block, block, f_send.at[2, d], f_recv.at[2, d], section, sibling)
        copy.start()
        outgoing.append(copy)
    for d in order:
        src = lax.rem(w - d + experts, experts)
        for n, place in ((1, g_core), (2, g_far)):
            block = held.at[src, place]
            remote(
                block, block, f_send.at[n, d], f_recv.at[n, d], section, sibling
            ).wait_recv()

    for e in range(experts):
        for q in range(WS):
            at = (e * WS + q) * part
            wide_a[at : at + part] = held[e, q, :part].astype(F32)
            wide_b[at : at + part] = held[e, q, part:].astype(F32)
    for j in range(pieces):
        cols = slice(j * LANES, (j + 1) * LANES)
        pieces_at = pl.ds(j, row_count, stride=pieces)
        rows_scaled[:, cols] = wide_b[pieces_at, :].astype(BF16)
        rows_in[:, cols] = wide_a[pieces_at, :].astype(BF16)
    upper = jnp.where(section >= sections // 2, 1, 0)
    own_cols = pl.ds(pl.multiple_of(upper * half, half), half)
    other_cols = pl.ds(pl.multiple_of((1 - upper) * half, half), half)
    copy = remote(
        rows_scaled.at[:, other_cols],
        scaled_other,
        p_send.at[0],
        p_recv.at[0],
        mirror,
        me,
    )
    copy.start()
    outgoing.append(copy)
    mirrored = [copy]

    loads[2].wait()
    loads[3].wait()
    loads[4].wait()
    gate_pre = dot(rows_in[...], w_gate[...])
    up_pre = dot(rows_in[...], w_up[...])
    sigmoid = jax.nn.sigmoid(gate_pre)
    activated = gate_pre * sigmoid
    slope = sigmoid * (1.0 + gate_pre * (1.0 - sigmoid))
    hidden = (activated * up_pre).astype(BF16)
    hidden_own[...] = hidden
    copy = remote(
        hidden_own, hidden_other, p_send.at[1], p_recv.at[1], mirror, me
    )
    copy.start()
    outgoing.append(copy)
    mirrored.append(copy)
    to_wire(wide_a, dot(hidden, w_down[...]), row_count)
    hidden_grad = dot(rows_scaled[...], w_down[...], ((1,), (1,)))
    grad_gate = (hidden_grad * up_pre * slope).astype(BF16)
    grad_up = (hidden_grad * activated).astype(BF16)
    transposed = ((1,), (1,))
    to_wire(
        wide_b,
        dot(grad_gate, w_gate[...], transposed) + dot(grad_up, w_up[...], transposed),
        row_count,
    )
    for q in range(WS):
        for e in range(experts):
            at = (e * WS + q) * part
            terms[q % 2, q // 2, e, :part] = wide_a[at : at + part].astype(BF16)
            terms[q % 2, q // 2, e, part:] = wide_b[at : at + part].astype(BF16)

    cores = []
    for n, side in enumerate((1 - x, x)):
        copy = remote(
            terms.at[1 - core, side],
            from_core.at[side],
            a_send.at[n],
            a_recv.at[n],
            section,
            sibling,
        )
        copy.start()
        outgoing.append(copy)
        cores.append(copy)
    cores[0].wait_recv()
    crossing = []
    for d in order:
        e = lax.rem(w + d, experts)
        to_x[e] = (
            terms[core, 1 - x, e].astype(F32) + from_core[1 - x, e].astype(F32)
        ).astype(BF16)
        copy = remote(
            to_x.at[e], from_x.at[e], b_send.at[d], b_recv.at[d], section, across
        )
        copy.start()
        outgoing.append(copy)
        crossing.append(copy)
    cores[1].wait_recv()
    returns = []
    for n, d in enumerate(order):
        e = lax.rem(w + d, experts)
        crossing[n].wait_recv()
        total = (
            terms[core, x, e].astype(F32)
            + from_core[x, e].astype(F32)
            + from_x[e].astype(F32)
        ).astype(BF16)
        if d == 0:
            returned[w] = total
        else:
            to_owner[e] = total
            copy = remote(
                to_owner.at[e],
                returned.at[w],
                c_send.at[d],
                c_recv.at[d],
                section,
                owner(e),
            )
            copy.start()
            outgoing.append(copy)
            returns.append(copy)

    down_own = dot(hidden_own[...], rows_scaled[:, own_cols], ((0,), (0,)))
    for copy in mirrored:
        copy.wait_recv()
    down_other = dot(hidden_other[...], scaled_other[...], ((0,), (0,)))
    down_grad_ref[0] = (
        down_own.astype(BF16).astype(F32) + down_other.astype(BF16).astype(F32)
    ).astype(BF16)

    for copy in returns:
        copy.wait_recv()
    for e in range(experts):
        wide_a[e * part : (e + 1) * part] = returned[e, :part].astype(F32)
        wide_b[e * part : (e + 1) * part] = returned[e, part:].astype(F32)
    if slots > experts * capacity:
        rest = slice(experts * part, slots * pieces)
        zero = jnp.zeros((slots * pieces - experts * part, LANES), F32)
        wide_a[rest] = zero
        wide_b[rest] = zero
    pick_narrow = pick[:, :slots].astype(BF16)
    gate_high = pick_gate[:, :slots].astype(BF16)
    left = pick_gate[:, :slots] - gate_high.astype(F32)
    gate_mid = left.astype(BF16)
    gate_low = (left - gate_mid.astype(F32)).astype(BF16)
    value = jnp.zeros((slots, LANES), F32)
    for j in range(pieces):
        cols = slice(j * LANES, (j + 1) * LANES)
        out = wide_a[pl.ds(j, slots, stride=pieces), :]
        narrow = out.astype(BF16)
        mixed_ref[:, cols] = (
            dot(gate_low, narrow) + dot(gate_mid, narrow) + dot(gate_high, narrow)
        ).astype(BF16)
        value += slot_cot[:, cols] * out
        grad = wide_b[pl.ds(j, slots, stride=pieces), :].astype(BF16)
        token_ref[:, cols] = dot(pick_narrow, grad).astype(BF16)
    column = jnp.sum(value, axis=1, keepdims=True)
    column = jnp.concatenate([column, jnp.zeros((LANES - slots, 1), F32)], axis=0)
    spread = pick * jnp.broadcast_to(column, (LANES, tok_count)).T
    for k in range(chosen):
        gate_grad_ref[:, k : k + 1] = jnp.sum(
            jnp.where(named[k], spread, 0.0), axis=1, keepdims=True
        )
    for copy in outgoing:
        copy.wait_send()


def body(sections, devices, tokens, cotangent, expert_ids, gates, w_gate, w_up, w_down):
    tok_count, width = tokens.shape
    capacity = tok_count // 24
    experts = devices // WS
    units = w_gate.shape[2]
    pieces = width // LANES
    part = capacity * pieces
    slots = -(-experts * capacity // 16) * 16
    rows = devices * capacity
    dma = pltpu.SemaphoreType.DMA
    anywhere = pl.BlockSpec(memory_space=pl.ANY)
    vmem = pl.BlockSpec(memory_space=pltpu.VMEM)
    return pl.pallas_call(
        functools.partial(kernel, sections, devices, capacity),
        out_shape=(
            jax.ShapeDtypeStruct((tok_count, width), BF16),
            jax.ShapeDtypeStruct((tok_count, width), BF16),
            jax.ShapeDtypeStruct(gates.shape, F32),
            jax.ShapeDtypeStruct((1, units, width // 2), BF16),
        ),
        in_specs=[anywhere, anywhere, vmem, vmem, anywhere, anywhere, anywhere],
        out_specs=(vmem, vmem, vmem, vmem),
        scratch_shapes=[
            pltpu.VMEM((tok_count, width), BF16),
            pltpu.VMEM((tok_count, width), BF16),
            pltpu.VMEM((width, units), BF16),
            pltpu.VMEM((width, units), BF16),
            pltpu.VMEM((units, width), BF16),
            pltpu.VMEM((rows * pieces, LANES), F32),
            pltpu.VMEM((rows * pieces, LANES), F32),
            pltpu.VMEM((slots, width), F32),
            pltpu.VMEM((experts, 2 * part, LANES), BF16),
            pltpu.VMEM((experts, WS, 2 * part, LANES), BF16),
            pltpu.VMEM((rows, width), BF16),
            pltpu.VMEM((rows, width), BF16),
            pltpu.VMEM((rows, units), BF16),
            pltpu.VMEM((rows, units), BF16),
            pltpu.VMEM((rows, width // 2), BF16),
            pltpu.VMEM((2, 2, experts, 2 * part, LANES), BF16),
            pltpu.VMEM((2, experts, 2 * part, LANES), BF16),
            pltpu.VMEM((experts, 2 * part, LANES), BF16),
            pltpu.VMEM((experts, 2 * part, LANES), BF16),
            pltpu.VMEM((experts, 2 * part, LANES), BF16),
            pltpu.VMEM((experts, 2 * part, LANES), BF16),
            dma((5,)),
            dma((experts,)),
            dma((experts,)),
            dma((3, experts)),
            dma((3, experts)),
            dma((2,)),
            dma((2,)),
            dma((2,)),
            dma((2,)),
            dma((experts,)),
            dma((experts,)),
            dma((experts,)),
            dma((experts,)),
        ],
        compiler_params=pltpu.CompilerParams(
            collective_id=0, has_side_effects=True, vmem_limit_bytes=48 << 20
        ),
        cost_estimate=pl.CostEstimate(
            flops=16 * rows * width * units,
            bytes_accessed=6 * width * units + 12 * tok_count * width,
            transcendentals=rows * units,
        ),
    )(tokens, cotangent, expert_ids, gates, w_gate, w_up, w_down)


def solution(mesh):
    rows = P(("pipe", "expert"), None)
    return jax.shard_map(
        functools.partial(body, mesh.shape["pipe"], mesh.shape["expert"]),
        mesh=mesh,
        in_specs=(
            rows,
            rows,
            rows,
            rows,
            P("pipe", None, "expert"),
            P("pipe", None, "expert"),
            P("pipe", "expert", None),
        ),
        out_specs=(rows, rows, rows, P("pipe", "expert", None)),
        check_vma=False,
    )
```

```python
import functools

import jax
import jax.numpy as jnp
from jax import lax
from jax.experimental import pallas as pl
from jax.experimental.pallas import tpu as pltpu
from jax.sharding import PartitionSpec as P

WS = 4
LANES = 128
BF16 = jnp.bfloat16
F32 = jnp.float32
MESH = pl.DeviceIdType.MESH


def dot(a, b, dims=((1,), (0,))):
    return lax.dot_general(a, b, (dims, ((), ())), preferred_element_type=F32)


def named_slots(ids, slots, experts, capacity):
    slot = lax.broadcasted_iota(jnp.int32, (slots, ids.shape[1]), 0)
    slot_expert = jnp.where(slot < experts * capacity, slot // capacity, -1)
    return [ids[k : k + 1, :] == slot_expert for k in range(ids.shape[0])]


def moe_kernel(
    sections,
    devices,
    capacity,
    tokens_hbm,
    cot_hbm,
    ids_ref,
    gates_ref,
    gate_hbm,
    up_hbm,
    down_hbm,
    returned_ref,
    pick_ref,
    pick_gate_ref,
    slot_cot_ref,
    down_grad_ref,
    tokens,
    cot,
    w_gate,
    w_up,
    w_down,
    wide_a,
    wide_b,
    sent,
    held,
    rows_in,
    rows_scaled,
    hidden_own,
    hidden_other,
    scaled_other,
    terms,
    from_core,
    to_x,
    from_x,
    to_owner,
    returned,
    load_sem,
    z_send,
    z_recv,
    f_send,
    f_recv,
    p_send,
    p_recv,
    a_send,
    a_recv,
    b_send,
    b_recv,
    c_send,
    c_recv,
):
    experts = devices // WS
    tok_count, width = tokens.shape
    pieces = width // LANES
    half = width // 2
    part = capacity * pieces
    slots = slot_cot_ref.shape[0]
    row_count = devices * capacity
    section = lax.axis_index("pipe")
    me = lax.axis_index("expert")
    w, g = me // WS, me % WS
    x, core = g // 2, g % 2
    mirror = sections - 1 - section
    sibling = w * WS + x * 2 + (1 - core)
    across = w * WS + (1 - x) * 2 + core
    transposed = ((1,), (1,))

    def owner(expert):
        return expert * WS + g

    def remote(src, dst, send, recv, pipe_pos, expert_pos):
        return pltpu.make_async_remote_copy(
            src_ref=src,
            dst_ref=dst,
            send_sem=send,
            recv_sem=recv,
            device_id=(pipe_pos, expert_pos),
            device_id_type=MESH,
        )

    outgoing = []

    def push(*args):
        copy = remote(*args)
        copy.start()
        outgoing.append(copy)
        return copy

    loads = [
        pltpu.make_async_copy(src, dst, load_sem.at[i])
        for i, (src, dst) in enumerate(
            [
                (tokens_hbm, tokens),
                (cot_hbm, cot),
                (gate_hbm.at[0], w_gate),
                (up_hbm.at[0], w_up),
                (down_hbm.at[0], w_down),
            ]
        )
    ]
    for load in loads:
        load.start()
    barrier = pltpu.get_barrier_semaphore()
    for d in range(1, experts):
        pl.semaphore_signal(
            barrier,
            inc=1,
            device_id=(section, owner(lax.rem(w + d, experts))),
            device_id_type=MESH,
        )
    for target in ((section, sibling), (section, across), (mirror, me)):
        pl.semaphore_signal(barrier, inc=1, device_id=target, device_id_type=MESH)

    ids = ids_ref[...]
    gates = gates_ref[...]
    named = named_slots(ids, slots, experts, capacity)
    match = jnp.zeros((slots, tok_count), F32)
    weight = jnp.zeros((slots, tok_count), F32)
    for k, here in enumerate(named):
        match += jnp.where(here, 1.0, 0.0)
        weight += jnp.where(here, gates[k : k + 1, :], 0.0)
    row_no = lax.broadcasted_iota(jnp.int32, (tok_count, tok_count), 0)
    col_no = lax.broadcasted_iota(jnp.int32, (tok_count, tok_count), 1)
    before = jnp.where(row_no < col_no, 1.0, 0.0).astype(BF16)
    earlier = dot(match.astype(BF16), before)
    slot = lax.broadcasted_iota(jnp.int32, (slots, tok_count), 0)
    slot_rank = (slot % capacity).astype(F32)
    pick = jnp.where((match > 0.5) & (earlier == slot_rank), 1.0, 0.0)
    pick_gate = pick * weight
    slot_gate = jnp.sum(pick_gate, axis=1, keepdims=True)
    pick_rows = pick.astype(BF16)

    def to_wire(scratch, values, count):
        for j in range(pieces):
            scratch[pl.ds(j, count, stride=pieces), :] = values[
                :, j * LANES : (j + 1) * LANES
            ]

    order = range(experts)
    far_first = range(experts - 1, 0, -1)
    spots = {
        "own": g,
        "core": x * 2 + (1 - core),
        "across": (1 - x) * 2 + core,
        "far": (1 - x) * 2 + (1 - core),
    }

    def dispatch(kind, scratch):
        for e in range(experts):
            sent[kind, e] = scratch[e * part : (e + 1) * part].astype(BF16)
        held[kind, 0, g] = sent[kind, w]

    def send_z(kind):
        for d in far_first:
            to = lax.rem(w + d, experts)
            push(
                sent.at[kind, to],
                held.at[kind, d, g],
                z_send.at[kind, d],
                z_recv.at[kind, d],
                section,
                owner(to),
            )

    def arrive(kind, hop, d, spot):
        block = held.at[kind, d, spots[spot]]
        if hop == 3:
            pair = (z_send.at[kind, d], z_recv.at[kind, d])
        else:
            pair = (f_send.at[kind, hop, d], f_recv.at[kind, hop, d])
        remote(block, block, *pair, section, sibling).wait_recv()

    def forward(kind, hop, d, spot, to):
        block = held.at[kind, d, spots[spot]]
        push(block, block, f_send.at[kind, hop, d], f_recv.at[kind, hop, d], section, to)

    def spread(kind):
        for d in order:
            if d:
                arrive(kind, 3, d, "own")
            forward(kind, 0, d, "own", across)
            forward(kind, 1, d, "own", sibling)

    def pass_on(kind):
        for d in order:
            arrive(kind, 0, d, "across")
            forward(kind, 2, d, "across", sibling)

    def collect(kind, scratch, rows):
        for d in order:
            arrive(kind, 1, d, "core")
            arrive(kind, 2, d, "far")
        for d in order:
            for q in range(WS):
                at = (d * WS + q) * part
                scratch[at : at + part] = held[kind, d, q].astype(F32)
        for j in range(pieces):
            rows[:, j * LANES : (j + 1) * LANES] = scratch[
                pl.ds(j, row_count, stride=pieces), :
            ].astype(BF16)

    def fold_cores(kind, scratch):
        for q in range(WS):
            for d in order:
                at = (d * WS + q) * part
                terms[kind, q % 2, q // 2, d] = scratch[at : at + part].astype(BF16)
        return [
            push(
                terms.at[kind, 1 - core, side],
                from_core.at[kind, side],
                a_send.at[kind, n],
                a_recv.at[kind, n],
                section,
                sibling,
            )
            for n, side in enumerate((1 - x, x))
        ]

    def fold_x(kind, cores):
        cores[0].wait_recv()
        crossing = []
        for d in far_first:
            to_x[kind, d] = (
                terms[kind, core, 1 - x, d].astype(F32)
                + from_core[kind, 1 - x, d].astype(F32)
            ).astype(BF16)
            crossing.append((d, push_x(kind, d)))
        to_x[kind, 0] = (
            terms[kind, core, 1 - x, 0].astype(F32)
            + from_core[kind, 1 - x, 0].astype(F32)
        ).astype(BF16)
        crossing.append((0, push_x(kind, 0)))
        cores[1].wait_recv()
        return crossing

    def push_x(kind, d):
        return push(
            to_x.at[kind, d],
            from_x.at[kind, d],
            b_send.at[kind, d],
            b_recv.at[kind, d],
            section,
            across,
        )

    def give_back(kind, crossing):
        returns = []
        for d, copy in crossing:
            copy.wait_recv()
            total = (
                terms[kind, core, x, d].astype(F32)
                + from_core[kind, x, d].astype(F32)
                + from_x[kind, d].astype(F32)
            ).astype(BF16)
            if d == 0:
                returned[kind, w] = total
            else:
                to_owner[kind, d] = total
                returns.append(
                    push(
                        to_owner.at[kind, d],
                        returned.at[kind, w],
                        c_send.at[kind, d],
                        c_recv.at[kind, d],
                        section,
                        owner(lax.rem(w + experts - d, experts)),
                    )
                )
        return returns

    loads[0].wait()
    to_wire(wide_a, dot(pick_rows, tokens[...]), slots)
    dispatch(0, wide_a)
    pl.semaphore_wait(barrier, experts + 2)
    send_z(0)
    loads[1].wait()
    cot_rows = dot(pick_rows, cot[...])
    to_wire(wide_b, slot_gate * cot_rows, slots)
    dispatch(1, wide_b)
    send_z(1)
    spread(0)
    slot_cot_ref[...] = cot_rows
    pick_ref[...] = pick
    pick_gate_ref[...] = pick_gate
    spread(1)
    pass_on(0)
    loads[2].wait()
    loads[3].wait()
    loads[4].wait()
    collect(0, wide_a, rows_in)
    gate_pre = dot(rows_in[...], w_gate[...], transposed)
    up_pre = dot(rows_in[...], w_up[...], transposed)
    sigmoid = jax.nn.sigmoid(gate_pre)
    activated = gate_pre * sigmoid
    slope = sigmoid * (1.0 + gate_pre * (1.0 - sigmoid))
    hidden = (activated * up_pre).astype(BF16)
    hidden_own[...] = hidden
    pass_on(1)
    to_wire(wide_a, dot(hidden, w_down[...]), row_count)
    out_cores = fold_cores(0, wide_a)
    mirrored = [push(hidden_own, hidden_other, p_send.at[1], p_recv.at[1], mirror, me)]

    collect(1, wide_b, rows_scaled)
    upper = jnp.where(section >= sections // 2, 1, 0)
    own_cols = pl.ds(pl.multiple_of(upper * half, half), half)
    other_cols = pl.ds(pl.multiple_of((1 - upper) * half, half), half)
    mirrored.append(
        push(
            rows_scaled.at[:, other_cols],
            scaled_other,
            p_send.at[0],
            p_recv.at[0],
            mirror,
            me,
        )
    )
    out_crossing = fold_x(0, out_cores)
    hidden_grad = dot(rows_scaled[...], w_down[...], transposed)
    grad_gate = (hidden_grad * up_pre * slope).astype(BF16)
    grad_up = (hidden_grad * activated).astype(BF16)
    to_wire(
        wide_b,
        dot(grad_gate, w_gate[...]) + dot(grad_up, w_up[...]),
        row_count,
    )
    grad_cores = fold_cores(1, wide_b)
    returns = give_back(0, out_crossing)
    grad_crossing = fold_x(1, grad_cores)
    down_own = dot(hidden_own[...], rows_scaled[:, own_cols], ((0,), (0,)))
    down_own = down_own.astype(BF16)
    returns += give_back(1, grad_crossing)
    for copy in mirrored:
        copy.wait_recv()
    down_other = dot(hidden_other[...], scaled_other[...], ((0,), (0,)))
    down_grad_ref[0] = (
        down_own.astype(F32) + down_other.astype(BF16).astype(F32)
    ).astype(BF16)
    for copy in returns:
        copy.wait_recv()
    returned_ref[...] = returned[...]
    for copy in outgoing:
        copy.wait_send()


def combine_kernel(
    experts,
    capacity,
    returned_ref,
    pick_ref,
    pick_gate_ref,
    slot_cot_ref,
    ids_ref,
    down_ref,
    mixed_ref,
    token_ref,
    gate_grad_ref,
    down_grad_ref,
    wide_a,
    wide_b,
):
    slots, width = slot_cot_ref.shape
    pieces = width // LANES
    part = capacity * pieces
    down_grad_ref[...] = down_ref[...]
    for e in range(experts):
        wide_a[e * part : (e + 1) * part] = returned_ref[0, e].astype(F32)
        wide_b[e * part : (e + 1) * part] = returned_ref[1, e].astype(F32)
    if slots > experts * capacity:
        rest = slice(experts * part, slots * pieces)
        zero = jnp.zeros((slots * pieces - experts * part, LANES), F32)
        wide_a[rest] = zero
        wide_b[rest] = zero
    pick = pick_ref[...]
    pick_gate = pick_gate_ref[...]
    turned = pick_gate.T
    high = turned.astype(BF16)
    left = turned - high.astype(F32)
    mid = left.astype(BF16)
    low = (left - mid.astype(F32)).astype(BF16)
    narrow_pick = pick.T.astype(BF16)
    value = jnp.zeros((slots, LANES), F32)
    outs = []
    grads = []
    for j in range(pieces):
        cols = slice(j * LANES, (j + 1) * LANES)
        out = wide_a[pl.ds(j, slots, stride=pieces), :]
        value += slot_cot_ref[:, cols] * out
        outs.append(out.astype(BF16))
        grads.append(wide_b[pl.ds(j, slots, stride=pieces), :].astype(BF16))
    for j in range(0, pieces, 4):
        cols = slice(j * LANES, (j + 4) * LANES)
        out = jnp.concatenate(outs[j : j + 4], axis=1)
        grad = jnp.concatenate(grads[j : j + 4], axis=1)
        mixed_ref[:, cols] = (dot(low, out) + dot(mid, out) + dot(high, out)).astype(
            BF16
        )
        token_ref[:, cols] = dot(narrow_pick, grad).astype(BF16)
    spread = pick * jnp.sum(value, axis=1, keepdims=True)
    for k, here in enumerate(named_slots(ids_ref[...], slots, experts, capacity)):
        gate_grad_ref[k : k + 1, :] = jnp.sum(
            jnp.where(here, spread, 0.0), axis=0, keepdims=True
        )


def body(sections, devices, tokens, cotangent, expert_ids, gates, w_gate, w_up, w_down):
    tok_count, width = tokens.shape
    capacity = tok_count // 24
    experts = devices // WS
    units = w_gate.shape[2]
    pieces = width // LANES
    part = capacity * pieces
    slots = -(-experts * capacity // 16) * 16
    rows = devices * capacity
    dma = pltpu.SemaphoreType.DMA
    far = pl.BlockSpec(memory_space=pltpu.HBM)
    vmem = pl.BlockSpec(memory_space=pltpu.VMEM)
    ids_turned = expert_ids.T
    returned, pick, pick_gate, slot_cot, down = pl.pallas_call(
        functools.partial(moe_kernel, sections, devices, capacity),
        out_shape=(
            jax.ShapeDtypeStruct((2, experts, part, LANES), BF16),
            jax.ShapeDtypeStruct((slots, tok_count), F32),
            jax.ShapeDtypeStruct((slots, tok_count), F32),
            jax.ShapeDtypeStruct((slots, width), F32),
            jax.ShapeDtypeStruct((1, units, width // 2), BF16),
        ),
        in_specs=[far, far, vmem, vmem, far, far, far],
        out_specs=(vmem,) * 5,
        scratch_shapes=[
            pltpu.VMEM((tok_count, width), BF16),
            pltpu.VMEM((tok_count, width), BF16),
            pltpu.VMEM((units, width), BF16),
            pltpu.VMEM((units, width), BF16),
            pltpu.VMEM((units, width), BF16),
            pltpu.VMEM((rows * pieces, LANES), F32),
            pltpu.VMEM((rows * pieces, LANES), F32),
            pltpu.VMEM((2, experts, part, LANES), BF16),
            pltpu.VMEM((2, experts, WS, part, LANES), BF16),
            pltpu.VMEM((rows, width), BF16),
            pltpu.VMEM((rows, width), BF16),
            pltpu.VMEM((rows, units), BF16),
            pltpu.VMEM((rows, units), BF16),
            pltpu.VMEM((rows, width // 2), BF16),
            pltpu.VMEM((2, 2, 2, experts, part, LANES), BF16),
            pltpu.VMEM((2, 2, experts, part, LANES), BF16),
            pltpu.VMEM((2, experts, part, LANES), BF16),
            pltpu.VMEM((2, experts, part, LANES), BF16),
            pltpu.VMEM((2, experts, part, LANES), BF16),
            pltpu.VMEM((2, experts, part, LANES), BF16),
            dma((5,)),
            dma((2, experts)),
            dma((2, experts)),
            dma((2, 3, experts)),
            dma((2, 3, experts)),
            dma((2,)),
            dma((2,)),
            dma((2, 2)),
            dma((2, 2)),
            dma((2, experts)),
            dma((2, experts)),
            dma((2, experts)),
            dma((2, experts)),
        ],
        compiler_params=pltpu.CompilerParams(
            collective_id=0, has_side_effects=True, vmem_limit_bytes=60 << 20
        ),
        cost_estimate=pl.CostEstimate(
            flops=16 * rows * width * units,
            bytes_accessed=6 * width * units + 12 * tok_count * width,
            transcendentals=rows * units,
        ),
    )(
        tokens,
        cotangent,
        ids_turned,
        gates.T,
        jnp.swapaxes(w_gate, 1, 2),
        jnp.swapaxes(w_up, 1, 2),
        w_down,
    )
    mixed_out, token_grad, gate_grad, down_grad = pl.pallas_call(
        functools.partial(combine_kernel, experts, capacity),
        out_shape=(
            jax.ShapeDtypeStruct((tok_count, width), BF16),
            jax.ShapeDtypeStruct((tok_count, width), BF16),
            jax.ShapeDtypeStruct(ids_turned.shape, F32),
            jax.ShapeDtypeStruct((1, units, width // 2), BF16),
        ),
        in_specs=[vmem] * 6,
        out_specs=(vmem,) * 4,
        scratch_shapes=[
            pltpu.VMEM((slots * pieces, LANES), F32),
            pltpu.VMEM((slots * pieces, LANES), F32),
        ],
        compiler_params=pltpu.CompilerParams(vmem_limit_bytes=60 << 20),
        cost_estimate=pl.CostEstimate(
            flops=8 * slots * width * tok_count,
            bytes_accessed=8 * tok_count * width,
            transcendentals=0,
        ),
    )(returned, pick, pick_gate, slot_cot, ids_turned, down)
    return mixed_out, token_grad, gate_grad.T, down_grad


def solution(mesh):
    rows = P(("pipe", "expert"), None)
    return jax.shard_map(
        functools.partial(body, mesh.shape["pipe"], mesh.shape["expert"]),
        mesh=mesh,
        in_specs=(
            rows,
            rows,
            rows,
            rows,
            P("pipe", None, "expert"),
            P("pipe", None, "expert"),
            P("pipe", "expert", None),
        ),
        out_specs=(rows, rows, rows, P("pipe", "expert", None)),
        check_vma=False,
    )
```

```python
import functools

import jax
import jax.numpy as jnp
from jax import lax
from jax.experimental import pallas as pl
from jax.experimental.pallas import tpu as pltpu
from jax.sharding import PartitionSpec as P

WS = 4
LANES = 128
BF16 = jnp.bfloat16
F32 = jnp.float32
MESH = pl.DeviceIdType.MESH


def dot(a, b, dims=((1,), (0,))):
    return lax.dot_general(a, b, (dims, ((), ())), preferred_element_type=F32)


def named_slots(ids, slots, experts, capacity):
    slot = lax.broadcasted_iota(jnp.int32, (slots, ids.shape[1]), 0)
    slot_expert = jnp.where(slot < experts * capacity, slot // capacity, -1)
    return [ids[k : k + 1, :] == slot_expert for k in range(ids.shape[0])]


def moe_kernel(
    sections,
    devices,
    capacity,
    tokens_hbm,
    cot_hbm,
    ids_ref,
    gates_ref,
    gate_hbm,
    up_hbm,
    down_hbm,
    returned_hbm,
    slot_hbm,
    down_grad_hbm,
    tokens,
    cot,
    w_gate,
    w_up,
    w_down,
    wide_a,
    wide_b,
    sent,
    held,
    rows_in,
    rows_scaled,
    hidden_own,
    hidden_other,
    scaled_other,
    terms,
    from_core,
    to_x,
    from_x,
    to_owner,
    returned,
    slot_info,
    down_grad,
    load_sem,
    store_sem,
    z_send,
    z_recv,
    f_send,
    f_recv,
    s_send,
    s_recv,
    p_send,
    p_recv,
    a_send,
    a_recv,
    b_send,
    b_recv,
    c_send,
    c_recv,
):
    experts = devices // WS
    tok_count, width = tokens.shape
    pieces = width // LANES
    half = width // 2
    part = capacity * pieces
    slots = slot_info.shape[0]
    row_count = devices * capacity
    section = lax.axis_index("pipe")
    me = lax.axis_index("expert")
    w, g = me // WS, me % WS
    x, core = g // 2, g % 2
    mirror = sections - 1 - section
    sibling = w * WS + x * 2 + (1 - core)
    across = w * WS + (1 - x) * 2 + core
    transposed = ((1,), (1,))

    def owner(expert):
        return expert * WS + g

    def remote(src, dst, send, recv, pipe_pos, expert_pos):
        return pltpu.make_async_remote_copy(
            src_ref=src,
            dst_ref=dst,
            send_sem=send,
            recv_sem=recv,
            device_id=(pipe_pos, expert_pos),
            device_id_type=MESH,
        )

    outgoing = []
    stores = []

    def push(*args):
        copy = remote(*args)
        copy.start()
        outgoing.append(copy)
        return copy

    loads = [
        pltpu.make_async_copy(src, dst, load_sem.at[i])
        for i, (src, dst) in enumerate(
            [
                (tokens_hbm, tokens),
                (cot_hbm, cot),
                (gate_hbm.at[0], w_gate),
                (up_hbm.at[0], w_up),
                (down_hbm.at[0], w_down),
            ]
        )
    ]
    loads[0].start()
    loads[1].start()
    barrier = pltpu.get_barrier_semaphore()
    for d in range(1, experts):
        pl.semaphore_signal(
            barrier,
            inc=1,
            device_id=(section, owner(lax.rem(w + d, experts))),
            device_id_type=MESH,
        )
    for target in ((section, sibling), (section, across), (mirror, me)):
        pl.semaphore_signal(barrier, inc=1, device_id=target, device_id_type=MESH)

    ids = ids_ref[...]
    gates = gates_ref[...]
    named = named_slots(ids, slots, experts, capacity)
    match = jnp.zeros((slots, tok_count), F32)
    weight = jnp.zeros((slots, tok_count), F32)
    for k, here in enumerate(named):
        match += jnp.where(here, 1.0, 0.0)
        weight += jnp.where(here, gates[k : k + 1, :], 0.0)
    row_no = lax.broadcasted_iota(jnp.int32, (tok_count, tok_count), 0)
    col_no = lax.broadcasted_iota(jnp.int32, (tok_count, tok_count), 1)
    before = jnp.where(row_no < col_no, 1.0, 0.0).astype(BF16)
    earlier = dot(match.astype(BF16), before)
    slot = lax.broadcasted_iota(jnp.int32, (slots, tok_count), 0)
    slot_rank = (slot % capacity).astype(F32)
    pick = jnp.where((match > 0.5) & (earlier == slot_rank), 1.0, 0.0)
    pick_gate = pick * weight
    slot_gate = jnp.sum(pick_gate, axis=1, keepdims=True)
    pick_rows = pick.astype(BF16)

    def to_wire(scratch, values, count):
        for j in range(pieces):
            scratch[pl.ds(j, count, stride=pieces), :] = values[
                :, j * LANES : (j + 1) * LANES
            ]

    order = range(experts)
    far_first = range(experts - 1, 0, -1)
    spots = {
        "core": x * 2 + (1 - core),
        "across": (1 - x) * 2 + core,
        "far": (1 - x) * 2 + (1 - core),
    }

    def dispatch(kind, scratch):
        for e in range(experts):
            sent[kind, e] = scratch[e * part : (e + 1) * part].astype(BF16)
        held[kind, g, 0] = sent[kind, w]

    def send_z(kind):
        for d in far_first:
            to = lax.rem(w + d, experts)
            push(
                sent.at[kind, to],
                held.at[kind, g, d],
                z_send.at[kind, d],
                z_recv.at[kind, d],
                section,
                owner(to),
            )

    def to_across(kind, d):
        block = held.at[kind, g, d]
        push(block, block, f_send.at[kind, d], f_recv.at[kind, d], section, across)

    def spread(kind):
        for d in range(1, experts):
            block = held.at[kind, g, d]
            remote(
                block, block, z_send.at[kind, d], z_recv.at[kind, d], section, sibling
            ).wait_recv()
            to_across(kind, d)
        block = held.at[kind, g]
        push(block, block, s_send.at[kind, 0], s_recv.at[kind, 0], section, sibling)

    def pass_on(kind):
        for d in order:
            block = held.at[kind, spots["across"], d]
            remote(
                block, block, f_send.at[kind, d], f_recv.at[kind, d], section, across
            ).wait_recv()
        block = held.at[kind, spots["across"]]
        push(block, block, s_send.at[kind, 1], s_recv.at[kind, 1], section, sibling)

    def collect(kind, scratch, rows):
        for n, spot in enumerate(("core", "far")):
            block = held.at[kind, spots[spot]]
            remote(
                block, block, s_send.at[kind, n], s_recv.at[kind, n], section, sibling
            ).wait_recv()
        for d in order:
            for q in range(WS):
                at = (d * WS + q) * part
                scratch[at : at + part] = held[kind, q, d].astype(F32)
        for j in range(pieces):
            rows[:, j * LANES : (j + 1) * LANES] = scratch[
                pl.ds(j, row_count, stride=pieces), :
            ].astype(BF16)

    def fold_cores(kind, scratch):
        for q in range(WS):
            for d in order:
                at = (d * WS + q) * part
                terms[kind, q % 2, q // 2, d] = scratch[at : at + part].astype(BF16)
        return [
            push(
                terms.at[kind, 1 - core, side],
                from_core.at[kind, side],
                a_send.at[kind, n],
                a_recv.at[kind, n],
                section,
                sibling,
            )
            for n, side in enumerate((1 - x, x))
        ]

    def fold_x(kind, cores):
        cores[0].wait_recv()
        crossing = []
        for d in far_first:
            to_x[kind, d] = (
                terms[kind, core, 1 - x, d].astype(F32)
                + from_core[kind, 1 - x, d].astype(F32)
            ).astype(BF16)
            crossing.append((d, push_x(kind, d)))
        to_x[kind, 0] = (
            terms[kind, core, 1 - x, 0].astype(F32)
            + from_core[kind, 1 - x, 0].astype(F32)
        ).astype(BF16)
        crossing.append((0, push_x(kind, 0)))
        cores[1].wait_recv()
        return crossing

    def push_x(kind, d):
        return push(
            to_x.at[kind, d],
            from_x.at[kind, d],
            b_send.at[kind, d],
            b_recv.at[kind, d],
            section,
            across,
        )

    def give_back(kind, crossing):
        returns = []
        for d, copy in crossing:
            copy.wait_recv()
            total = (
                terms[kind, core, x, d].astype(F32)
                + from_core[kind, x, d].astype(F32)
                + from_x[kind, d].astype(F32)
            ).astype(BF16)
            if d == 0:
                returned[kind] = total
                local = pltpu.make_async_copy(
                    returned.at[kind], returned_hbm.at[kind, w], store_sem.at[1 + kind]
                )
                local.start()
                stores.append(local)
            else:
                to_owner[kind, d] = total
                returns.append(
                    push(
                        to_owner.at[kind, d],
                        returned_hbm.at[kind, w],
                        c_send.at[kind, d],
                        c_recv.at[kind, d],
                        section,
                        owner(lax.rem(w + experts - d, experts)),
                    )
                )
        return returns

    loads[0].wait()
    to_wire(wide_a, dot(pick_rows, tokens[...]), slots)
    dispatch(0, wide_a)
    pl.semaphore_wait(barrier, experts + 2)
    send_z(0)
    to_across(0, 0)
    for load in loads[2:]:
        load.start()
    loads[1].wait()
    cot_rows = dot(pick_rows, cot[...])
    to_wire(wide_b, slot_gate * cot_rows, slots)
    dispatch(1, wide_b)
    send_z(1)
    to_across(1, 0)
    slot_info[:, :width] = cot_rows
    slot_info[:, width : width + tok_count] = pick
    slot_info[:, width + tok_count :] = pick_gate
    slot_store = pltpu.make_async_copy(slot_info, slot_hbm, store_sem.at[0])
    slot_store.start()
    spread(0)
    spread(1)
    pass_on(0)
    loads[2].wait()
    loads[3].wait()
    loads[4].wait()
    collect(0, wide_a, rows_in)
    gate_pre = dot(rows_in[...], w_gate[...], transposed)
    up_pre = dot(rows_in[...], w_up[...], transposed)
    sigmoid = jax.nn.sigmoid(gate_pre)
    activated = gate_pre * sigmoid
    slope = sigmoid * (1.0 + gate_pre * (1.0 - sigmoid))
    hidden = (activated * up_pre).astype(BF16)
    hidden_own[...] = hidden
    pass_on(1)
    to_wire(wide_a, dot(hidden, w_down[...]), row_count)
    out_cores = fold_cores(0, wide_a)
    mirrored = [push(hidden_own, hidden_other, p_send.at[1], p_recv.at[1], mirror, me)]

    collect(1, wide_b, rows_scaled)
    upper = jnp.where(section >= sections // 2, 1, 0)
    own_cols = pl.ds(pl.multiple_of(upper * half, half), half)
    other_cols = pl.ds(pl.multiple_of((1 - upper) * half, half), half)
    mirrored.append(
        push(
            rows_scaled.at[:, other_cols],
            scaled_other,
            p_send.at[0],
            p_recv.at[0],
            mirror,
            me,
        )
    )
    out_crossing = fold_x(0, out_cores)
    hidden_grad = dot(rows_scaled[...], w_down[...], transposed)
    grad_gate = (hidden_grad * up_pre * slope).astype(BF16)
    grad_up = (hidden_grad * activated).astype(BF16)
    to_wire(
        wide_b,
        dot(grad_gate, w_gate[...]) + dot(grad_up, w_up[...]),
        row_count,
    )
    grad_cores = fold_cores(1, wide_b)
    returns = give_back(0, out_crossing)
    grad_crossing = fold_x(1, grad_cores)
    down_own = dot(hidden_own[...], rows_scaled[:, own_cols], ((0,), (0,)))
    down_own = down_own.astype(BF16)
    returns += give_back(1, grad_crossing)
    for copy in mirrored:
        copy.wait_recv()
    down_other = dot(hidden_other[...], scaled_other[...], ((0,), (0,)))
    down_grad[0] = (
        down_own.astype(F32) + down_other.astype(BF16).astype(F32)
    ).astype(BF16)
    down_store = pltpu.make_async_copy(down_grad, down_grad_hbm, store_sem.at[3])
    down_store.start()
    for store in stores + [slot_store, down_store]:
        store.wait()
    for copy in returns:
        copy.wait_recv()
    for copy in outgoing:
        copy.wait_send()


def combine_kernel(
    experts,
    capacity,
    returned_hbm,
    slot_hbm,
    ids_ref,
    down_hbm,
    mixed_hbm,
    token_hbm,
    gate_grad_ref,
    down_grad_hbm,
    returned,
    slot_info,
    down,
    mixed,
    token,
    wide_a,
    wide_b,
    load_sem,
    down_sem,
    mixed_sem,
    token_sem,
):
    slots = slot_info.shape[0]
    tok_count, width = mixed.shape
    pieces = width // LANES
    part = capacity * pieces
    loads = [
        pltpu.make_async_copy(returned_hbm, returned, load_sem.at[0]),
        pltpu.make_async_copy(slot_hbm, slot_info, load_sem.at[1]),
        pltpu.make_async_copy(down_hbm, down, load_sem.at[2]),
    ]
    for load in loads:
        load.start()
    named = named_slots(ids_ref[...], slots, experts, capacity)
    loads[0].wait()
    for e in range(experts):
        wide_a[e * part : (e + 1) * part] = returned[0, e].astype(F32)
        wide_b[e * part : (e + 1) * part] = returned[1, e].astype(F32)
    if slots > experts * capacity:
        rest = slice(experts * part, slots * pieces)
        zero = jnp.zeros((slots * pieces - experts * part, LANES), F32)
        wide_a[rest] = zero
        wide_b[rest] = zero
    loads[1].wait()
    pick = slot_info[:, width : width + tok_count]
    pick_gate = slot_info[:, width + tok_count :]
    turned = pick_gate.T
    high = turned.astype(BF16)
    left = turned - high.astype(F32)
    mid = left.astype(BF16)
    low = (left - mid.astype(F32)).astype(BF16)
    narrow_pick = pick.T.astype(BF16)
    value = jnp.zeros((slots, LANES), F32)
    stores = []

    def write(src, dst, sem):
        store = pltpu.make_async_copy(src, dst, sem)
        store.start()
        stores.append(store)

    span = 4 if pieces % 4 == 0 else 1
    for n, first in enumerate(range(0, pieces, span)):
        cols = slice(first * LANES, (first + span) * LANES)
        grads = [
            wide_b[pl.ds(j, slots, stride=pieces), :].astype(BF16)
            for j in range(first, first + span)
        ]
        grad = jnp.concatenate(grads, axis=1)
        token[:, cols] = dot(narrow_pick, grad).astype(BF16)
        write(token.at[:, cols], token_hbm.at[:, cols], token_sem.at[n])
    loads[2].wait()
    write(down, down_grad_hbm, down_sem)
    for n, first in enumerate(range(0, pieces, span)):
        cols = slice(first * LANES, (first + span) * LANES)
        outs = [
            wide_a[pl.ds(j, slots, stride=pieces), :]
            for j in range(first, first + span)
        ]
        for j, out in enumerate(outs):
            at = (first + j) * LANES
            value += slot_info[:, at : at + LANES] * out
        out = jnp.concatenate([out.astype(BF16) for out in outs], axis=1)
        mixed[:, cols] = (dot(low, out) + dot(mid, out) + dot(high, out)).astype(BF16)
        write(mixed.at[:, cols], mixed_hbm.at[:, cols], mixed_sem.at[n])
    spread = pick * jnp.sum(value, axis=1, keepdims=True)
    for k, here in enumerate(named):
        gate_grad_ref[k : k + 1, :] = jnp.sum(
            jnp.where(here, spread, 0.0), axis=0, keepdims=True
        )
    for store in stores:
        store.wait()


def body(sections, devices, tokens, cotangent, expert_ids, gates, w_gate, w_up, w_down):
    tok_count, width = tokens.shape
    capacity = tok_count // 24
    experts = devices // WS
    units = w_gate.shape[2]
    pieces = width // LANES
    part = capacity * pieces
    slots = -(-experts * capacity // 16) * 16
    rows = devices * capacity
    dma = pltpu.SemaphoreType.DMA
    anywhere = pl.BlockSpec(memory_space=pl.ANY)
    vmem = pl.BlockSpec(memory_space=pltpu.VMEM)
    ids_turned = expert_ids.T
    returned, slot_info, down = pl.pallas_call(
        functools.partial(moe_kernel, sections, devices, capacity),
        out_shape=(
            jax.ShapeDtypeStruct((2, experts, part, LANES), BF16),
            jax.ShapeDtypeStruct((slots, width + 2 * tok_count), F32),
            jax.ShapeDtypeStruct((1, units, width // 2), BF16),
        ),
        in_specs=[anywhere, anywhere, vmem, vmem, anywhere, anywhere, anywhere],
        out_specs=(anywhere,) * 3,
        scratch_shapes=[
            pltpu.VMEM((tok_count, width), BF16),
            pltpu.VMEM((tok_count, width), BF16),
            pltpu.VMEM((units, width), BF16),
            pltpu.VMEM((units, width), BF16),
            pltpu.VMEM((units, width), BF16),
            pltpu.VMEM((rows * pieces, LANES), F32),
            pltpu.VMEM((rows * pieces, LANES), F32),
            pltpu.VMEM((2, experts, part, LANES), BF16),
            pltpu.VMEM((2, WS, experts, part, LANES), BF16),
            pltpu.VMEM((rows, width), BF16),
            pltpu.VMEM((rows, width), BF16),
            pltpu.VMEM((rows, units), BF16),
            pltpu.VMEM((rows, units), BF16),
            pltpu.VMEM((rows, width // 2), BF16),
            pltpu.VMEM((2, 2, 2, experts, part, LANES), BF16),
            pltpu.VMEM((2, 2, experts, part, LANES), BF16),
            pltpu.VMEM((2, experts, part, LANES), BF16),
            pltpu.VMEM((2, experts, part, LANES), BF16),
            pltpu.VMEM((2, experts, part, LANES), BF16),
            pltpu.VMEM((2, part, LANES), BF16),
            pltpu.VMEM((slots, width + 2 * tok_count), F32),
            pltpu.VMEM((1, units, width // 2), BF16),
            dma((5,)),
            dma((4,)),
            dma((2, experts)),
            dma((2, experts)),
            dma((2, experts)),
            dma((2, experts)),
            dma((2, 2)),
            dma((2, 2)),
            dma((2,)),
            dma((2,)),
            dma((2, 2)),
            dma((2, 2)),
            dma((2, experts)),
            dma((2, experts)),
            dma((2, experts)),
            dma((2, experts)),
        ],
        compiler_params=pltpu.CompilerParams(
            collective_id=0, has_side_effects=True, vmem_limit_bytes=60 << 20
        ),
        cost_estimate=pl.CostEstimate(
            flops=16 * rows * width * units,
            bytes_accessed=6 * width * units + 12 * tok_count * width,
            transcendentals=rows * units,
        ),
    )(
        tokens,
        cotangent,
        ids_turned,
        gates.T,
        jnp.swapaxes(w_gate, 1, 2),
        jnp.swapaxes(w_up, 1, 2),
        w_down,
    )
    mixed_out, token_grad, gate_grad, down_grad = pl.pallas_call(
        functools.partial(combine_kernel, experts, capacity),
        out_shape=(
            jax.ShapeDtypeStruct((tok_count, width), BF16),
            jax.ShapeDtypeStruct((tok_count, width), BF16),
            jax.ShapeDtypeStruct(ids_turned.shape, F32),
            jax.ShapeDtypeStruct((1, units, width // 2), BF16),
        ),
        in_specs=[anywhere, anywhere, vmem, anywhere],
        out_specs=(anywhere, anywhere, vmem, anywhere),
        scratch_shapes=[
            pltpu.VMEM((2, experts, part, LANES), BF16),
            pltpu.VMEM((slots, width + 2 * tok_count), F32),
            pltpu.VMEM((1, units, width // 2), BF16),
            pltpu.VMEM((tok_count, width), BF16),
            pltpu.VMEM((tok_count, width), BF16),
            pltpu.VMEM((slots * pieces, LANES), F32),
            pltpu.VMEM((slots * pieces, LANES), F32),
            dma((3,)),
            dma(()),
            dma((pieces,)),
            dma((pieces,)),
        ],
        compiler_params=pltpu.CompilerParams(vmem_limit_bytes=60 << 20),
        cost_estimate=pl.CostEstimate(
            flops=8 * slots * width * tok_count,
            bytes_accessed=8 * tok_count * width,
            transcendentals=0,
        ),
    )(returned, slot_info, ids_turned, down)
    return mixed_out, token_grad, gate_grad.T, down_grad


def solution(mesh):
    rows = P(("pipe", "expert"), None)
    return jax.shard_map(
        functools.partial(body, mesh.shape["pipe"], mesh.shape["expert"]),
        mesh=mesh,
        in_specs=(
            rows,
            rows,
            rows,
            rows,
            P("pipe", None, "expert"),
            P("pipe", None, "expert"),
            P("pipe", "expert", None),
        ),
        out_specs=(rows, rows, rows, P("pipe", "expert", None)),
        check_vma=False,
    )
```

```python
import functools

import jax
import jax.numpy as jnp
from jax import lax
from jax.experimental import pallas as pl
from jax.experimental.pallas import tpu as pltpu
from jax.sharding import PartitionSpec as P

WS = 4
LANES = 128
BF16 = jnp.bfloat16
F32 = jnp.float32
MESH = pl.DeviceIdType.MESH


def dot(a, b, dims=((1,), (0,))):
    return lax.dot_general(a, b, (dims, ((), ())), preferred_element_type=F32)


def named_slots(ids, slots, experts, capacity):
    slot = lax.broadcasted_iota(jnp.int32, (slots, ids.shape[1]), 0)
    slot_expert = jnp.where(slot < experts * capacity, slot // capacity, -1)
    return [ids[k : k + 1, :] == slot_expert for k in range(ids.shape[0])]


def moe_kernel(
    sections,
    devices,
    capacity,
    tokens_hbm,
    cot_hbm,
    ids_ref,
    gates_ref,
    gate_hbm,
    up_hbm,
    down_hbm,
    returned_hbm,
    slot_hbm,
    down_grad_hbm,
    tokens,
    cot,
    w_both,
    w_down,
    wide_a,
    wide_b,
    sent,
    held,
    rows_in,
    rows_scaled,
    hidden_own,
    hidden_other,
    scaled_other,
    terms,
    from_core,
    to_x,
    from_x,
    to_owner,
    returned,
    slot_info,
    down_grad,
    load_sem,
    store_sem,
    z_send,
    z_recv,
    f_send,
    f_recv,
    s_send,
    s_recv,
    p_send,
    p_recv,
    a_send,
    a_recv,
    b_send,
    b_recv,
    c_send,
    c_recv,
):
    experts = devices // WS
    tok_count, width = tokens.shape
    pieces = width // LANES
    half = width // 2
    units = w_down.shape[0]
    part = capacity * pieces
    slots = slot_info.shape[0]
    row_count = devices * capacity
    section = lax.axis_index("pipe")
    me = lax.axis_index("expert")
    w, g = me // WS, me % WS
    x, core = g // 2, g % 2
    mirror = sections - 1 - section
    sibling = w * WS + x * 2 + (1 - core)
    across = w * WS + (1 - x) * 2 + core
    transposed = ((1,), (1,))

    def owner(expert):
        return expert * WS + g

    def remote(src, dst, send, recv, pipe_pos, expert_pos):
        return pltpu.make_async_remote_copy(
            src_ref=src,
            dst_ref=dst,
            send_sem=send,
            recv_sem=recv,
            device_id=(pipe_pos, expert_pos),
            device_id_type=MESH,
        )

    outgoing = []
    stores = []

    def push(*args):
        copy = remote(*args)
        copy.start()
        outgoing.append(copy)
        return copy

    loads = [
        pltpu.make_async_copy(src, dst, load_sem.at[i])
        for i, (src, dst) in enumerate(
            [
                (tokens_hbm, tokens),
                (cot_hbm, cot),
                (gate_hbm.at[0], w_both.at[:units]),
                (up_hbm.at[0], w_both.at[units:]),
                (down_hbm.at[0], w_down),
            ]
        )
    ]
    loads[0].start()
    loads[1].start()
    barrier = pltpu.get_barrier_semaphore()
    for d in range(1, experts):
        pl.semaphore_signal(
            barrier,
            inc=1,
            device_id=(section, owner(lax.rem(w + d, experts))),
            device_id_type=MESH,
        )
    for target in ((section, sibling), (section, across), (mirror, me)):
        pl.semaphore_signal(barrier, inc=1, device_id=target, device_id_type=MESH)

    ids = ids_ref[...]
    gates = gates_ref[...]
    named = named_slots(ids, slots, experts, capacity)
    match = jnp.zeros((slots, tok_count), F32)
    weight = jnp.zeros((slots, tok_count), F32)
    for k, here in enumerate(named):
        match += jnp.where(here, 1.0, 0.0)
        weight += jnp.where(here, gates[k : k + 1, :], 0.0)
    row_no = lax.broadcasted_iota(jnp.int32, (tok_count, tok_count), 0)
    col_no = lax.broadcasted_iota(jnp.int32, (tok_count, tok_count), 1)
    before = jnp.where(row_no < col_no, 1.0, 0.0).astype(BF16)
    earlier = dot(match.astype(BF16), before)
    slot = lax.broadcasted_iota(jnp.int32, (slots, tok_count), 0)
    slot_rank = (slot % capacity).astype(F32)
    pick = jnp.where((match > 0.5) & (earlier == slot_rank), 1.0, 0.0)
    pick_gate = pick * weight
    slot_gate = jnp.sum(pick_gate, axis=1, keepdims=True)
    pick_rows = pick.astype(BF16)

    def to_wire(scratch, values, count):
        for j in range(pieces):
            scratch[pl.ds(j, count, stride=pieces), :] = values[
                :, j * LANES : (j + 1) * LANES
            ]

    def product_to_wire(scratch, left, right):
        span = 4 if pieces % 4 == 0 else 1
        for first in range(0, pieces, span):
            values = dot(left, right[:, first * LANES : (first + span) * LANES])
            for j in range(span):
                scratch[pl.ds(first + j, row_count, stride=pieces), :] = values[
                    :, j * LANES : (j + 1) * LANES
                ]

    order = range(experts)
    far_first = range(experts - 1, 0, -1)
    spots = {
        "core": x * 2 + (1 - core),
        "across": (1 - x) * 2 + core,
        "far": (1 - x) * 2 + (1 - core),
    }

    def dispatch(kind, scratch):
        for e in range(experts):
            sent[kind, e] = scratch[e * part : (e + 1) * part].astype(BF16)
        held[kind, g, 0] = sent[kind, w]

    def send_z(kind):
        for d in far_first:
            to = lax.rem(w + d, experts)
            push(
                sent.at[kind, to],
                held.at[kind, g, d],
                z_send.at[kind, d],
                z_recv.at[kind, d],
                section,
                owner(to),
            )

    def to_across(kind, d):
        block = held.at[kind, g, d]
        push(block, block, f_send.at[kind, d], f_recv.at[kind, d], section, across)

    def spread(kind):
        for d in range(1, experts):
            block = held.at[kind, g, d]
            remote(
                block, block, z_send.at[kind, d], z_recv.at[kind, d], section, sibling
            ).wait_recv()
            to_across(kind, d)
        block = held.at[kind, g]
        push(block, block, s_send.at[kind, 0], s_recv.at[kind, 0], section, sibling)

    def pass_on(kind):
        for d in order:
            block = held.at[kind, spots["across"], d]
            remote(
                block, block, f_send.at[kind, d], f_recv.at[kind, d], section, across
            ).wait_recv()
        block = held.at[kind, spots["across"]]
        push(block, block, s_send.at[kind, 1], s_recv.at[kind, 1], section, sibling)

    def collect(kind, scratch, rows):
        for n, spot in enumerate(("core", "far")):
            block = held.at[kind, spots[spot]]
            remote(
                block, block, s_send.at[kind, n], s_recv.at[kind, n], section, sibling
            ).wait_recv()
        for d in order:
            for q in range(WS):
                at = (d * WS + q) * part
                scratch[at : at + part] = held[kind, q, d].astype(F32)
        for j in range(pieces):
            rows[:, j * LANES : (j + 1) * LANES] = scratch[
                pl.ds(j, row_count, stride=pieces), :
            ].astype(BF16)

    def fold_cores(kind, scratch):
        for q in range(WS):
            for d in order:
                at = (d * WS + q) * part
                terms[kind, q % 2, q // 2, d] = scratch[at : at + part].astype(BF16)
        return [
            push(
                terms.at[kind, 1 - core, side],
                from_core.at[kind, side],
                a_send.at[kind, n],
                a_recv.at[kind, n],
                section,
                sibling,
            )
            for n, side in enumerate((1 - x, x))
        ]

    def fold_x(kind, cores):
        cores[0].wait_recv()
        crossing = []
        for d in far_first:
            to_x[kind, d] = (
                terms[kind, core, 1 - x, d].astype(F32)
                + from_core[kind, 1 - x, d].astype(F32)
            ).astype(BF16)
            crossing.append((d, push_x(kind, d)))
        to_x[kind, 0] = (
            terms[kind, core, 1 - x, 0].astype(F32)
            + from_core[kind, 1 - x, 0].astype(F32)
        ).astype(BF16)
        crossing.append((0, push_x(kind, 0)))
        cores[1].wait_recv()
        return crossing

    def push_x(kind, d):
        return push(
            to_x.at[kind, d],
            from_x.at[kind, d],
            b_send.at[kind, d],
            b_recv.at[kind, d],
            section,
            across,
        )

    def give_back(kind, crossing):
        returns = []
        for d, copy in crossing:
            copy.wait_recv()
            total = (
                terms[kind, core, x, d].astype(F32)
                + from_core[kind, x, d].astype(F32)
                + from_x[kind, d].astype(F32)
            ).astype(BF16)
            if d == 0:
                returned[kind] = total
                local = pltpu.make_async_copy(
                    returned.at[kind], returned_hbm.at[kind, w], store_sem.at[1 + kind]
                )
                local.start()
                stores.append(local)
            else:
                to_owner[kind, d] = total
                returns.append(
                    push(
                        to_owner.at[kind, d],
                        returned_hbm.at[kind, w],
                        c_send.at[kind, d],
                        c_recv.at[kind, d],
                        section,
                        owner(lax.rem(w + experts - d, experts)),
                    )
                )
        return returns

    loads[0].wait()
    to_wire(wide_a, dot(pick_rows, tokens[...]), slots)
    dispatch(0, wide_a)
    pl.semaphore_wait(barrier, experts + 2)
    send_z(0)
    to_across(0, 0)
    for load in loads[2:]:
        load.start()
    loads[1].wait()
    cot_rows = dot(pick_rows, cot[...])
    to_wire(wide_b, slot_gate * cot_rows, slots)
    dispatch(1, wide_b)
    send_z(1)
    to_across(1, 0)
    slot_info[:, :width] = cot_rows
    slot_info[:, width : width + tok_count] = pick
    slot_info[:, width + tok_count :] = pick_gate
    slot_store = pltpu.make_async_copy(slot_info, slot_hbm, store_sem.at[0])
    slot_store.start()
    spread(0)
    spread(1)
    pass_on(0)
    loads[2].wait()
    loads[3].wait()
    loads[4].wait()
    collect(0, wide_a, rows_in)
    both_pre = dot(rows_in[...], w_both[...], transposed)
    gate_pre = both_pre[:, :units]
    up_pre = both_pre[:, units:]
    sigmoid = jax.nn.sigmoid(gate_pre)
    activated = gate_pre * sigmoid
    slope = sigmoid * (1.0 + gate_pre * (1.0 - sigmoid))
    hidden = (activated * up_pre).astype(BF16)
    hidden_own[...] = hidden
    pass_on(1)
    product_to_wire(wide_a, hidden, w_down)
    out_cores = fold_cores(0, wide_a)
    mirrored = [push(hidden_own, hidden_other, p_send.at[1], p_recv.at[1], mirror, me)]

    collect(1, wide_b, rows_scaled)
    upper = jnp.where(section >= sections // 2, 1, 0)
    own_cols = pl.ds(pl.multiple_of(upper * half, half), half)
    other_cols = pl.ds(pl.multiple_of((1 - upper) * half, half), half)
    mirrored.append(
        push(
            rows_scaled.at[:, other_cols],
            scaled_other,
            p_send.at[0],
            p_recv.at[0],
            mirror,
            me,
        )
    )
    out_crossing = fold_x(0, out_cores)
    hidden_grad = dot(rows_scaled[...], w_down[...], transposed)
    grad_gate = (hidden_grad * up_pre * slope).astype(BF16)
    grad_up = (hidden_grad * activated).astype(BF16)
    product_to_wire(wide_b, jnp.concatenate([grad_gate, grad_up], axis=1), w_both)
    grad_cores = fold_cores(1, wide_b)
    returns = give_back(0, out_crossing)
    grad_crossing = fold_x(1, grad_cores)
    down_own = dot(hidden_own[...], rows_scaled[:, own_cols], ((0,), (0,)))
    down_own = down_own.astype(BF16)
    returns += give_back(1, grad_crossing)
    for copy in mirrored:
        copy.wait_recv()
    down_other = dot(hidden_other[...], scaled_other[...], ((0,), (0,)))
    down_grad[0] = (
        down_own.astype(F32) + down_other.astype(BF16).astype(F32)
    ).astype(BF16)
    down_store = pltpu.make_async_copy(down_grad, down_grad_hbm, store_sem.at[3])
    down_store.start()
    for store in stores + [slot_store, down_store]:
        store.wait()
    for copy in returns:
        copy.wait_recv()
    for copy in outgoing:
        copy.wait_send()


def combine_kernel(
    experts,
    capacity,
    returned_ref,
    slot_ref,
    ids_ref,
    down_ref,
    mixed_ref,
    token_ref,
    gate_grad_ref,
    down_grad_ref,
    wide_a,
    wide_b,
):
    slots = slot_ref.shape[0]
    tok_count, width = mixed_ref.shape
    pieces = width // LANES
    part = capacity * pieces
    down_grad_ref[...] = down_ref[...]
    for e in range(experts):
        wide_a[e * part : (e + 1) * part] = returned_ref[0, e].astype(F32)
        wide_b[e * part : (e + 1) * part] = returned_ref[1, e].astype(F32)
    if slots > experts * capacity:
        rest = slice(experts * part, slots * pieces)
        zero = jnp.zeros((slots * pieces - experts * part, LANES), F32)
        wide_a[rest] = zero
        wide_b[rest] = zero
    pick = slot_ref[:, width : width + tok_count]
    pick_gate = slot_ref[:, width + tok_count :]
    high = pick_gate.astype(BF16).astype(F32)
    mid = (pick_gate - high).astype(BF16).astype(F32)
    low = pick_gate - high - mid
    terms = jnp.concatenate([low, mid, high], axis=0).T.astype(BF16)
    narrow_pick = pick.T.astype(BF16)
    value = jnp.zeros((slots, LANES), F32)
    span = 4 if pieces % 4 == 0 else 1
    for first in range(0, pieces, span):
        cols = slice(first * LANES, (first + span) * LANES)
        outs = []
        grads = []
        for j in range(first, first + span):
            out = wide_a[pl.ds(j, slots, stride=pieces), :]
            value += slot_ref[:, j * LANES : (j + 1) * LANES] * out
            outs.append(out.astype(BF16))
            grads.append(wide_b[pl.ds(j, slots, stride=pieces), :].astype(BF16))
        out = jnp.concatenate(outs, axis=1)
        mixed_ref[:, cols] = dot(terms, jnp.concatenate([out] * 3, axis=0)).astype(BF16)
        token_ref[:, cols] = dot(narrow_pick, jnp.concatenate(grads, axis=1)).astype(
            BF16
        )
    spread = pick * jnp.sum(value, axis=1, keepdims=True)
    for k, here in enumerate(named_slots(ids_ref[...], slots, experts, capacity)):
        gate_grad_ref[k : k + 1, :] = jnp.sum(
            jnp.where(here, spread, 0.0), axis=0, keepdims=True
        )


def body(sections, devices, tokens, cotangent, expert_ids, gates, w_gate, w_up, w_down):
    tok_count, width = tokens.shape
    capacity = tok_count // 24
    experts = devices // WS
    units = w_gate.shape[2]
    pieces = width // LANES
    part = capacity * pieces
    slots = -(-experts * capacity // 16) * 16
    rows = devices * capacity
    dma = pltpu.SemaphoreType.DMA
    anywhere = pl.BlockSpec(memory_space=pl.ANY)
    vmem = pl.BlockSpec(memory_space=pltpu.VMEM)
    ids_turned = expert_ids.T
    returned, slot_info, down = pl.pallas_call(
        functools.partial(moe_kernel, sections, devices, capacity),
        out_shape=(
            jax.ShapeDtypeStruct((2, experts, part, LANES), BF16),
            jax.ShapeDtypeStruct((slots, width + 2 * tok_count), F32),
            jax.ShapeDtypeStruct((1, units, width // 2), BF16),
        ),
        in_specs=[anywhere, anywhere, vmem, vmem, anywhere, anywhere, anywhere],
        out_specs=(anywhere,) * 3,
        scratch_shapes=[
            pltpu.VMEM((tok_count, width), BF16),
            pltpu.VMEM((tok_count, width), BF16),
            pltpu.VMEM((2 * units, width), BF16),
            pltpu.VMEM((units, width), BF16),
            pltpu.VMEM((rows * pieces, LANES), F32),
            pltpu.VMEM((rows * pieces, LANES), F32),
            pltpu.VMEM((2, experts, part, LANES), BF16),
            pltpu.VMEM((2, WS, experts, part, LANES), BF16),
            pltpu.VMEM((rows, width), BF16),
            pltpu.VMEM((rows, width), BF16),
            pltpu.VMEM((rows, units), BF16),
            pltpu.VMEM((rows, units), BF16),
            pltpu.VMEM((rows, width // 2), BF16),
            pltpu.VMEM((2, 2, 2, experts, part, LANES), BF16),
            pltpu.VMEM((2, 2, experts, part, LANES), BF16),
            pltpu.VMEM((2, experts, part, LANES), BF16),
            pltpu.VMEM((2, experts, part, LANES), BF16),
            pltpu.VMEM((2, experts, part, LANES), BF16),
            pltpu.VMEM((2, part, LANES), BF16),
            pltpu.VMEM((slots, width + 2 * tok_count), F32),
            pltpu.VMEM((1, units, width // 2), BF16),
            dma((5,)),
            dma((4,)),
            dma((2, experts)),
            dma((2, experts)),
            dma((2, experts)),
            dma((2, experts)),
            dma((2, 2)),
            dma((2, 2)),
            dma((2,)),
            dma((2,)),
            dma((2, 2)),
            dma((2, 2)),
            dma((2, experts)),
            dma((2, experts)),
            dma((2, experts)),
            dma((2, experts)),
        ],
        compiler_params=pltpu.CompilerParams(
            collective_id=0, has_side_effects=True, vmem_limit_bytes=60 << 20
        ),
        cost_estimate=pl.CostEstimate(
            flops=16 * rows * width * units,
            bytes_accessed=6 * width * units + 12 * tok_count * width,
            transcendentals=rows * units,
        ),
    )(
        tokens,
        cotangent,
        ids_turned,
        gates.T,
        jnp.swapaxes(w_gate, 1, 2),
        jnp.swapaxes(w_up, 1, 2),
        w_down,
    )
    mixed_out, token_grad, gate_grad, down_grad = pl.pallas_call(
        functools.partial(combine_kernel, experts, capacity),
        out_shape=(
            jax.ShapeDtypeStruct((tok_count, width), BF16),
            jax.ShapeDtypeStruct((tok_count, width), BF16),
            jax.ShapeDtypeStruct(ids_turned.shape, F32),
            jax.ShapeDtypeStruct((1, units, width // 2), BF16),
        ),
        in_specs=[vmem] * 4,
        out_specs=(vmem,) * 4,
        scratch_shapes=[
            pltpu.VMEM((slots * pieces, LANES), F32),
            pltpu.VMEM((slots * pieces, LANES), F32),
        ],
        compiler_params=pltpu.CompilerParams(vmem_limit_bytes=60 << 20),
        cost_estimate=pl.CostEstimate(
            flops=8 * slots * width * tok_count,
            bytes_accessed=8 * tok_count * width,
            transcendentals=0,
        ),
    )(returned, slot_info, ids_turned, down)
    return mixed_out, token_grad, gate_grad.T, down_grad


def solution(mesh):
    rows = P(("pipe", "expert"), None)
    return jax.shard_map(
        functools.partial(body, mesh.shape["pipe"], mesh.shape["expert"]),
        mesh=mesh,
        in_specs=(
            rows,
            rows,
            rows,
            rows,
            P("pipe", None, "expert"),
            P("pipe", None, "expert"),
            P("pipe", "expert", None),
        ),
        out_specs=(rows, rows, rows, P("pipe", "expert", None)),
        check_vma=False,
    )
```

```python
import functools

import jax
import jax.numpy as jnp
from jax import lax
from jax.experimental import pallas as pl
from jax.experimental.pallas import tpu as pltpu
from jax.sharding import PartitionSpec as P

WS = 4
LANES = 128
BF16 = jnp.bfloat16
F32 = jnp.float32
MESH = pl.DeviceIdType.MESH


def dot(a, b, dims=((1,), (0,))):
    return lax.dot_general(a, b, (dims, ((), ())), preferred_element_type=F32)


def named_slots(ids, slots, experts, capacity):
    slot = lax.broadcasted_iota(jnp.int32, (slots, ids.shape[1]), 0)
    slot_expert = jnp.where(slot < experts * capacity, slot // capacity, -1)
    return [ids[k : k + 1, :] == slot_expert for k in range(ids.shape[0])]


def moe_kernel(
    sections,
    devices,
    capacity,
    tokens_hbm,
    cot_hbm,
    ids_hbm,
    gates_hbm,
    gate_hbm,
    up_hbm,
    down_hbm,
    returned_hbm,
    slot_hbm,
    down_grad_hbm,
    ids_ref,
    gates_ref,
    tokens,
    cot,
    w_both,
    w_down,
    wide_a,
    wide_b,
    sent,
    held,
    rows_in,
    rows_scaled,
    hidden_own,
    hidden_other,
    scaled_other,
    terms,
    from_core,
    to_x,
    from_x,
    to_owner,
    returned,
    slot_info,
    down_grad,
    load_sem,
    store_sem,
    z_send,
    z_recv,
    f_send,
    f_recv,
    s_send,
    s_recv,
    p_send,
    p_recv,
    a_send,
    a_recv,
    b_send,
    b_recv,
    c_send,
    c_recv,
):
    experts = devices // WS
    tok_count, width = tokens.shape
    pieces = width // LANES
    half = width // 2
    units = w_down.shape[0]
    part = capacity * pieces
    slots = slot_info.shape[0]
    row_count = devices * capacity
    section = lax.axis_index("pipe")
    me = lax.axis_index("expert")
    w, g = me // WS, me % WS
    x, core = g // 2, g % 2
    mirror = sections - 1 - section
    sibling = w * WS + x * 2 + (1 - core)
    across = w * WS + (1 - x) * 2 + core
    transposed = ((1,), (1,))

    def owner(expert):
        return expert * WS + g

    def remote(src, dst, send, recv, pipe_pos, expert_pos):
        return pltpu.make_async_remote_copy(
            src_ref=src,
            dst_ref=dst,
            send_sem=send,
            recv_sem=recv,
            device_id=(pipe_pos, expert_pos),
            device_id_type=MESH,
        )

    outgoing = []
    stores = []

    def push(*args):
        copy = remote(*args)
        copy.start()
        outgoing.append(copy)
        return copy

    loads = [
        pltpu.make_async_copy(src, dst, load_sem.at[i])
        for i, (src, dst) in enumerate(
            [
                (tokens_hbm, tokens),
                (cot_hbm, cot),
                (gate_hbm.at[0], w_both.at[:units]),
                (up_hbm.at[0], w_both.at[units:]),
                (down_hbm.at[0], w_down),
                (ids_hbm, ids_ref),
                (gates_hbm, gates_ref),
            ]
        )
    ]
    for i in (5, 6, 0, 1):
        loads[i].start()
    barrier = pltpu.get_barrier_semaphore()
    for d in range(1, experts):
        pl.semaphore_signal(
            barrier,
            inc=1,
            device_id=(section, owner(lax.rem(w + d, experts))),
            device_id_type=MESH,
        )
    for target in ((section, sibling), (section, across), (mirror, me)):
        pl.semaphore_signal(barrier, inc=1, device_id=target, device_id_type=MESH)

    row_no = lax.broadcasted_iota(jnp.int32, (tok_count, tok_count), 0)
    col_no = lax.broadcasted_iota(jnp.int32, (tok_count, tok_count), 1)
    before = jnp.where(row_no < col_no, 1.0, 0.0).astype(BF16)
    loads[5].wait()
    loads[6].wait()
    ids = ids_ref[...]
    gates = gates_ref[...]
    named = named_slots(ids, slots, experts, capacity)
    match = jnp.zeros((slots, tok_count), F32)
    weight = jnp.zeros((slots, tok_count), F32)
    for k, here in enumerate(named):
        match += jnp.where(here, 1.0, 0.0)
        weight += jnp.where(here, gates[k : k + 1, :], 0.0)
    earlier = dot(match.astype(BF16), before)
    slot = lax.broadcasted_iota(jnp.int32, (slots, tok_count), 0)
    slot_rank = (slot % capacity).astype(F32)
    pick = jnp.where((match > 0.5) & (earlier == slot_rank), 1.0, 0.0)
    pick_gate = pick * weight
    slot_gate = jnp.sum(pick_gate, axis=1, keepdims=True)
    pick_rows = pick.astype(BF16)

    def to_wire(scratch, values, count):
        for j in range(pieces):
            scratch[pl.ds(j, count, stride=pieces), :] = values[
                :, j * LANES : (j + 1) * LANES
            ]

    def product_to_wire(scratch, left, right):
        span = 4 if pieces % 4 == 0 else 1
        for first in range(0, pieces, span):
            values = dot(left, right[:, first * LANES : (first + span) * LANES])
            for j in range(span):
                scratch[pl.ds(first + j, row_count, stride=pieces), :] = values[
                    :, j * LANES : (j + 1) * LANES
                ]

    order = range(experts)
    far_first = range(experts - 1, 0, -1)
    spots = {
        "core": x * 2 + (1 - core),
        "across": (1 - x) * 2 + core,
        "far": (1 - x) * 2 + (1 - core),
    }

    def dispatch(kind, scratch):
        for e in range(experts):
            sent[kind, e] = scratch[e * part : (e + 1) * part].astype(BF16)
        held[kind, g, 0] = sent[kind, w]

    def send_z(kind):
        for d in far_first:
            to = lax.rem(w + d, experts)
            push(
                sent.at[kind, to],
                held.at[kind, g, d],
                z_send.at[kind, d],
                z_recv.at[kind, d],
                section,
                owner(to),
            )

    def to_across(kind, d):
        block = held.at[kind, g, d]
        push(block, block, f_send.at[kind, d], f_recv.at[kind, d], section, across)

    def spread(kind):
        for d in far_first:
            block = held.at[kind, g, d]
            remote(
                block, block, z_send.at[kind, d], z_recv.at[kind, d], section, sibling
            ).wait_recv()
            to_across(kind, d)
        block = held.at[kind, g]
        push(block, block, s_send.at[kind, 0], s_recv.at[kind, 0], section, sibling)

    def pass_on(kind):
        for d in (0, *far_first):
            block = held.at[kind, spots["across"], d]
            remote(
                block, block, f_send.at[kind, d], f_recv.at[kind, d], section, across
            ).wait_recv()
        block = held.at[kind, spots["across"]]
        push(block, block, s_send.at[kind, 1], s_recv.at[kind, 1], section, sibling)

    def collect(kind, scratch, rows):
        for n, spot in enumerate(("core", "far")):
            block = held.at[kind, spots[spot]]
            remote(
                block, block, s_send.at[kind, n], s_recv.at[kind, n], section, sibling
            ).wait_recv()
        for d in order:
            for q in range(WS):
                at = (d * WS + q) * part
                scratch[at : at + part] = held[kind, q, d].astype(F32)
        for j in range(pieces):
            rows[:, j * LANES : (j + 1) * LANES] = scratch[
                pl.ds(j, row_count, stride=pieces), :
            ].astype(BF16)

    def fold_cores(kind, scratch):
        for q in range(WS):
            for d in order:
                at = (d * WS + q) * part
                terms[kind, q % 2, q // 2, d] = scratch[at : at + part].astype(BF16)
        return [
            push(
                terms.at[kind, 1 - core, side],
                from_core.at[kind, side],
                a_send.at[kind, n],
                a_recv.at[kind, n],
                section,
                sibling,
            )
            for n, side in enumerate((1 - x, x))
        ]

    def fold_x(kind, cores):
        cores[0].wait_recv()
        crossing = []
        for d in far_first:
            to_x[kind, d] = (
                terms[kind, core, 1 - x, d].astype(F32)
                + from_core[kind, 1 - x, d].astype(F32)
            ).astype(BF16)
            crossing.append((d, push_x(kind, d)))
        to_x[kind, 0] = (
            terms[kind, core, 1 - x, 0].astype(F32)
            + from_core[kind, 1 - x, 0].astype(F32)
        ).astype(BF16)
        crossing.append((0, push_x(kind, 0)))
        cores[1].wait_recv()
        return crossing

    def push_x(kind, d):
        return push(
            to_x.at[kind, d],
            from_x.at[kind, d],
            b_send.at[kind, d],
            b_recv.at[kind, d],
            section,
            across,
        )

    def give_back(kind, crossing):
        returns = []
        for d, copy in crossing:
            copy.wait_recv()
            total = (
                terms[kind, core, x, d].astype(F32)
                + from_core[kind, x, d].astype(F32)
                + from_x[kind, d].astype(F32)
            ).astype(BF16)
            if d == 0:
                returned[kind] = total
                local = pltpu.make_async_copy(
                    returned.at[kind], returned_hbm.at[kind, w], store_sem.at[1 + kind]
                )
                local.start()
                stores.append(local)
            else:
                to_owner[kind, d] = total
                returns.append(
                    push(
                        to_owner.at[kind, d],
                        returned_hbm.at[kind, w],
                        c_send.at[kind, d],
                        c_recv.at[kind, d],
                        section,
                        owner(lax.rem(w + experts - d, experts)),
                    )
                )
        return returns

    loads[0].wait()
    to_wire(wide_a, dot(pick_rows, tokens[...]), slots)
    dispatch(0, wide_a)
    pl.semaphore_wait(barrier, experts + 2)
    send_z(0)
    to_across(0, 0)
    for load in loads[2:5]:
        load.start()
    loads[1].wait()
    cot_rows = dot(pick_rows, cot[...])
    to_wire(wide_b, slot_gate * cot_rows, slots)
    dispatch(1, wide_b)
    send_z(1)
    to_across(1, 0)
    slot_info[:, :width] = cot_rows
    slot_info[:, width : width + tok_count] = pick
    slot_info[:, width + tok_count :] = pick_gate
    slot_store = pltpu.make_async_copy(slot_info, slot_hbm, store_sem.at[0])
    slot_store.start()
    spread(0)
    spread(1)
    pass_on(0)
    loads[2].wait()
    loads[3].wait()
    loads[4].wait()
    collect(0, wide_a, rows_in)
    both_pre = dot(rows_in[...], w_both[...], transposed)
    gate_pre = both_pre[:, :units]
    up_pre = both_pre[:, units:]
    sigmoid = jax.nn.sigmoid(gate_pre)
    activated = gate_pre * sigmoid
    slope = sigmoid * (1.0 + gate_pre * (1.0 - sigmoid))
    hidden = (activated * up_pre).astype(BF16)
    hidden_own[...] = hidden
    pass_on(1)
    product_to_wire(wide_a, hidden, w_down)
    out_cores = fold_cores(0, wide_a)
    mirrored = [push(hidden_own, hidden_other, p_send.at[1], p_recv.at[1], mirror, me)]

    collect(1, wide_b, rows_scaled)
    upper = jnp.where(section >= sections // 2, 1, 0)
    own_cols = pl.ds(pl.multiple_of(upper * half, half), half)
    other_cols = pl.ds(pl.multiple_of((1 - upper) * half, half), half)
    mirrored.append(
        push(
            rows_scaled.at[:, other_cols],
            scaled_other,
            p_send.at[0],
            p_recv.at[0],
            mirror,
            me,
        )
    )
    out_crossing = fold_x(0, out_cores)
    hidden_grad = dot(rows_scaled[...], w_down[...], transposed)
    grad_gate = (hidden_grad * up_pre * slope).astype(BF16)
    grad_up = (hidden_grad * activated).astype(BF16)
    product_to_wire(wide_b, jnp.concatenate([grad_gate, grad_up], axis=1), w_both)
    grad_cores = fold_cores(1, wide_b)
    returns = give_back(0, out_crossing)
    grad_crossing = fold_x(1, grad_cores)
    down_own = dot(hidden_own[...], rows_scaled[:, own_cols], ((0,), (0,)))
    down_own = down_own.astype(BF16)
    returns += give_back(1, grad_crossing)
    for copy in mirrored:
        copy.wait_recv()
    down_other = dot(hidden_other[...], scaled_other[...], ((0,), (0,)))
    down_grad[0] = (
        down_own.astype(F32) + down_other.astype(BF16).astype(F32)
    ).astype(BF16)
    down_store = pltpu.make_async_copy(down_grad, down_grad_hbm, store_sem.at[3])
    down_store.start()
    for store in stores + [slot_store, down_store]:
        store.wait()
    for copy in returns:
        copy.wait_recv()
    for copy in outgoing:
        copy.wait_send()


def combine_kernel(
    experts,
    capacity,
    returned_ref,
    slot_ref,
    ids_ref,
    down_ref,
    mixed_ref,
    token_ref,
    gate_grad_ref,
    down_grad_ref,
    wide_a,
    wide_b,
):
    slots = slot_ref.shape[0]
    tok_count, width = mixed_ref.shape
    pieces = width // LANES
    part = capacity * pieces
    down_grad_ref[...] = down_ref[...]
    for e in range(experts):
        wide_a[e * part : (e + 1) * part] = returned_ref[0, e].astype(F32)
        wide_b[e * part : (e + 1) * part] = returned_ref[1, e].astype(F32)
    if slots > experts * capacity:
        rest = slice(experts * part, slots * pieces)
        zero = jnp.zeros((slots * pieces - experts * part, LANES), F32)
        wide_a[rest] = zero
        wide_b[rest] = zero
    pick = slot_ref[:, width : width + tok_count]
    pick_gate = slot_ref[:, width + tok_count :]
    high = pick_gate.astype(BF16).astype(F32)
    mid = (pick_gate - high).astype(BF16).astype(F32)
    low = pick_gate - high - mid
    terms = jnp.concatenate([low, mid, high], axis=0).T.astype(BF16)
    narrow_pick = pick.T.astype(BF16)
    value = jnp.zeros((slots, LANES), F32)
    span = 4 if pieces % 4 == 0 else 1
    for first in range(0, pieces, span):
        cols = slice(first * LANES, (first + span) * LANES)
        outs = []
        grads = []
        for j in range(first, first + span):
            out = wide_a[pl.ds(j, slots, stride=pieces), :]
            value += slot_ref[:, j * LANES : (j + 1) * LANES] * out
            outs.append(out.astype(BF16))
            grads.append(wide_b[pl.ds(j, slots, stride=pieces), :].astype(BF16))
        out = jnp.concatenate(outs, axis=1)
        mixed_ref[:, cols] = dot(terms, jnp.concatenate([out] * 3, axis=0)).astype(BF16)
        token_ref[:, cols] = dot(narrow_pick, jnp.concatenate(grads, axis=1)).astype(
            BF16
        )
    spread = pick * jnp.sum(value, axis=1, keepdims=True)
    for k, here in enumerate(named_slots(ids_ref[...], slots, experts, capacity)):
        gate_grad_ref[k : k + 1, :] = jnp.sum(
            jnp.where(here, spread, 0.0), axis=0, keepdims=True
        )


def body(sections, devices, tokens, cotangent, expert_ids, gates, w_gate, w_up, w_down):
    tok_count, width = tokens.shape
    capacity = tok_count // 24
    experts = devices // WS
    units = w_gate.shape[2]
    pieces = width // LANES
    part = capacity * pieces
    slots = -(-experts * capacity // 16) * 16
    rows = devices * capacity
    dma = pltpu.SemaphoreType.DMA
    anywhere = pl.BlockSpec(memory_space=pl.ANY)
    vmem = pl.BlockSpec(memory_space=pltpu.VMEM)
    ids_turned = expert_ids.T
    returned, slot_info, down = pl.pallas_call(
        functools.partial(moe_kernel, sections, devices, capacity),
        out_shape=(
            jax.ShapeDtypeStruct((2, experts, part, LANES), BF16),
            jax.ShapeDtypeStruct((slots, width + 2 * tok_count), F32),
            jax.ShapeDtypeStruct((1, units, width // 2), BF16),
        ),
        in_specs=[anywhere] * 7,
        out_specs=(anywhere,) * 3,
        scratch_shapes=[
            pltpu.VMEM(ids_turned.shape, jnp.int32),
            pltpu.VMEM(ids_turned.shape, F32),
            pltpu.VMEM((tok_count, width), BF16),
            pltpu.VMEM((tok_count, width), BF16),
            pltpu.VMEM((2 * units, width), BF16),
            pltpu.VMEM((units, width), BF16),
            pltpu.VMEM((rows * pieces, LANES), F32),
            pltpu.VMEM((rows * pieces, LANES), F32),
            pltpu.VMEM((2, experts, part, LANES), BF16),
            pltpu.VMEM((2, WS, experts, part, LANES), BF16),
            pltpu.VMEM((rows, width), BF16),
            pltpu.VMEM((rows, width), BF16),
            pltpu.VMEM((rows, units), BF16),
            pltpu.VMEM((rows, units), BF16),
            pltpu.VMEM((rows, width // 2), BF16),
            pltpu.VMEM((2, 2, 2, experts, part, LANES), BF16),
            pltpu.VMEM((2, 2, experts, part, LANES), BF16),
            pltpu.VMEM((2, experts, part, LANES), BF16),
            pltpu.VMEM((2, experts, part, LANES), BF16),
            pltpu.VMEM((2, experts, part, LANES), BF16),
            pltpu.VMEM((2, part, LANES), BF16),
            pltpu.VMEM((slots, width + 2 * tok_count), F32),
            pltpu.VMEM((1, units, width // 2), BF16),
            dma((7,)),
            dma((4,)),
            dma((2, experts)),
            dma((2, experts)),
            dma((2, experts)),
            dma((2, experts)),
            dma((2, 2)),
            dma((2, 2)),
            dma((2,)),
            dma((2,)),
            dma((2, 2)),
            dma((2, 2)),
            dma((2, experts)),
            dma((2, experts)),
            dma((2, experts)),
            dma((2, experts)),
        ],
        compiler_params=pltpu.CompilerParams(
            collective_id=0, has_side_effects=True, vmem_limit_bytes=60 << 20
        ),
        cost_estimate=pl.CostEstimate(
            flops=16 * rows * width * units,
            bytes_accessed=6 * width * units + 12 * tok_count * width,
            transcendentals=rows * units,
        ),
    )(
        tokens,
        cotangent,
        ids_turned,
        gates.T,
        jnp.swapaxes(w_gate, 1, 2),
        jnp.swapaxes(w_up, 1, 2),
        w_down,
    )
    mixed_out, token_grad, gate_grad, down_grad = pl.pallas_call(
        functools.partial(combine_kernel, experts, capacity),
        out_shape=(
            jax.ShapeDtypeStruct((tok_count, width), BF16),
            jax.ShapeDtypeStruct((tok_count, width), BF16),
            jax.ShapeDtypeStruct(ids_turned.shape, F32),
            jax.ShapeDtypeStruct((1, units, width // 2), BF16),
        ),
        in_specs=[vmem] * 4,
        out_specs=(vmem,) * 4,
        scratch_shapes=[
            pltpu.VMEM((slots * pieces, LANES), F32),
            pltpu.VMEM((slots * pieces, LANES), F32),
        ],
        compiler_params=pltpu.CompilerParams(vmem_limit_bytes=60 << 20),
        cost_estimate=pl.CostEstimate(
            flops=8 * slots * width * tok_count,
            bytes_accessed=8 * tok_count * width,
            transcendentals=0,
        ),
    )(returned, slot_info, ids_turned, down)
    return mixed_out, token_grad, gate_grad.T, down_grad


def solution(mesh):
    rows = P(("pipe", "expert"), None)
    return jax.shard_map(
        functools.partial(body, mesh.shape["pipe"], mesh.shape["expert"]),
        mesh=mesh,
        in_specs=(
            rows,
            rows,
            rows,
            rows,
            P("pipe", None, "expert"),
            P("pipe", None, "expert"),
            P("pipe", "expert", None),
        ),
        out_specs=(rows, rows, rows, P("pipe", "expert", None)),
        check_vma=False,
    )
```

```python
import functools

import jax
import jax.numpy as jnp
from jax import lax
from jax.experimental import pallas as pl
from jax.experimental.pallas import tpu as pltpu
from jax.sharding import PartitionSpec as P

WS = 4
LANES = 128
BF16 = jnp.bfloat16
F32 = jnp.float32
MESH = pl.DeviceIdType.MESH


def dot(a, b, dims=((1,), (0,))):
    return lax.dot_general(a, b, (dims, ((), ())), preferred_element_type=F32)


def named_slots(ids, slots, experts, capacity):
    slot = lax.broadcasted_iota(jnp.int32, (slots, ids.shape[1]), 0)
    slot_expert = jnp.where(slot < experts * capacity, slot // capacity, -1)
    return [ids[k : k + 1, :] == slot_expert for k in range(ids.shape[0])]


def moe_kernel(
    sections,
    devices,
    capacity,
    tokens_hbm,
    cot_hbm,
    ids_hbm,
    gates_hbm,
    gate_hbm,
    up_hbm,
    down_hbm,
    returned_hbm,
    slot_hbm,
    down_grad_hbm,
    ids_ref,
    gates_ref,
    tokens,
    cot,
    w_both,
    w_down,
    wide_a,
    wide_b,
    sent,
    held,
    rows_in,
    rows_scaled,
    hidden_own,
    hidden_other,
    scaled_other,
    terms,
    from_core,
    to_x,
    from_x,
    to_owner,
    returned,
    slot_info,
    down_grad,
    load_sem,
    store_sem,
    z_send,
    z_recv,
    f_send,
    f_recv,
    s_send,
    s_recv,
    p_send,
    p_recv,
    a_send,
    a_recv,
    b_send,
    b_recv,
    c_send,
    c_recv,
):
    experts = devices // WS
    tok_count, width = tokens.shape
    pieces = width // LANES
    half = width // 2
    units = w_down.shape[0]
    part = capacity * pieces
    slots = slot_info.shape[0]
    row_count = devices * capacity
    section = lax.axis_index("pipe")
    me = lax.axis_index("expert")
    w, g = me // WS, me % WS
    x, core = g // 2, g % 2
    mirror = sections - 1 - section
    sibling = w * WS + x * 2 + (1 - core)
    across = w * WS + (1 - x) * 2 + core
    transposed = ((1,), (1,))

    def owner(expert):
        return expert * WS + g

    def remote(src, dst, send, recv, pipe_pos, expert_pos):
        return pltpu.make_async_remote_copy(
            src_ref=src,
            dst_ref=dst,
            send_sem=send,
            recv_sem=recv,
            device_id=(pipe_pos, expert_pos),
            device_id_type=MESH,
        )

    outgoing = []
    stores = []

    def push(*args):
        copy = remote(*args)
        copy.start()
        outgoing.append(copy)
        return copy

    loads = [
        pltpu.make_async_copy(src, dst, load_sem.at[i])
        for i, (src, dst) in enumerate(
            [
                (tokens_hbm, tokens),
                (cot_hbm, cot),
                (gate_hbm.at[0], w_both.at[:units]),
                (up_hbm.at[0], w_both.at[units:]),
                (down_hbm.at[0], w_down),
                (ids_hbm, ids_ref),
                (gates_hbm, gates_ref),
            ]
        )
    ]
    for i in (5, 6, 0, 1):
        loads[i].start()
    barrier = pltpu.get_barrier_semaphore()
    for d in range(1, experts):
        pl.semaphore_signal(
            barrier,
            inc=1,
            device_id=(section, owner(lax.rem(w + d, experts))),
            device_id_type=MESH,
        )
    for target in ((section, sibling), (section, across), (mirror, me)):
        pl.semaphore_signal(barrier, inc=1, device_id=target, device_id_type=MESH)

    row_no = lax.broadcasted_iota(jnp.int32, (tok_count, tok_count), 0)
    col_no = lax.broadcasted_iota(jnp.int32, (tok_count, tok_count), 1)
    before = jnp.where(row_no < col_no, 1.0, 0.0).astype(BF16)
    loads[5].wait()
    loads[6].wait()
    ids = ids_ref[...]
    gates = gates_ref[...]
    named = named_slots(ids, slots, experts, capacity)
    match = jnp.zeros((slots, tok_count), F32)
    weight = jnp.zeros((slots, tok_count), F32)
    for k, here in enumerate(named):
        match += jnp.where(here, 1.0, 0.0)
        weight += jnp.where(here, gates[k : k + 1, :], 0.0)
    earlier = dot(match.astype(BF16), before)
    slot = lax.broadcasted_iota(jnp.int32, (slots, tok_count), 0)
    slot_rank = (slot % capacity).astype(F32)
    pick = jnp.where((match > 0.5) & (earlier == slot_rank), 1.0, 0.0)
    pick_gate = pick * weight
    slot_gate = jnp.sum(pick_gate, axis=1, keepdims=True)
    pick_rows = pick.astype(BF16)

    def to_wire(scratch, values, count):
        for j in range(pieces):
            scratch[pl.ds(j, count, stride=pieces), :] = values[
                :, j * LANES : (j + 1) * LANES
            ]

    def product_to_wire(scratch, left, right):
        span = 4 if pieces % 4 == 0 else 1
        for first in range(0, pieces, span):
            values = dot(left, right[:, first * LANES : (first + span) * LANES])
            for j in range(span):
                scratch[pl.ds(first + j, row_count, stride=pieces), :] = values[
                    :, j * LANES : (j + 1) * LANES
                ]

    order = range(experts)
    far_first = range(experts - 1, 0, -1)
    spots = {
        "core": x * 2 + (1 - core),
        "across": (1 - x) * 2 + core,
        "far": (1 - x) * 2 + (1 - core),
    }

    def dispatch(kind, scratch):
        for e in range(experts):
            sent[kind, e] = scratch[e * part : (e + 1) * part].astype(BF16)
        held[kind, g, 0] = sent[kind, w]

    def send_z(kind):
        for d in far_first:
            to = lax.rem(w + d, experts)
            push(
                sent.at[kind, to],
                held.at[kind, g, d],
                z_send.at[kind, d],
                z_recv.at[kind, d],
                section,
                owner(to),
            )

    def to_across(kind, d):
        block = held.at[kind, g, d]
        push(block, block, f_send.at[kind, d], f_recv.at[kind, d], section, across)

    def spread(kind):
        for d in far_first:
            block = held.at[kind, g, d]
            remote(
                block, block, z_send.at[kind, d], z_recv.at[kind, d], section, sibling
            ).wait_recv()
            to_across(kind, d)
        block = held.at[kind, g]
        push(block, block, s_send.at[kind, 0], s_recv.at[kind, 0], section, sibling)

    def pass_on(kind):
        for d in (0, *far_first):
            block = held.at[kind, spots["across"], d]
            remote(
                block, block, f_send.at[kind, d], f_recv.at[kind, d], section, across
            ).wait_recv()
        block = held.at[kind, spots["across"]]
        push(block, block, s_send.at[kind, 1], s_recv.at[kind, 1], section, sibling)

    def collect(kind, scratch, rows):
        for n, spot in enumerate(("core", "far")):
            block = held.at[kind, spots[spot]]
            remote(
                block, block, s_send.at[kind, n], s_recv.at[kind, n], section, sibling
            ).wait_recv()
        for d in order:
            for q in range(WS):
                at = (d * WS + q) * part
                scratch[at : at + part] = held[kind, q, d].astype(F32)
        for j in range(pieces):
            rows[:, j * LANES : (j + 1) * LANES] = scratch[
                pl.ds(j, row_count, stride=pieces), :
            ].astype(BF16)

    def fold_cores(kind, scratch):
        for q in range(WS):
            for d in order:
                at = (d * WS + q) * part
                terms[kind, q % 2, q // 2, d] = scratch[at : at + part].astype(BF16)
        return [
            push(
                terms.at[kind, 1 - core, side],
                from_core.at[kind, side],
                a_send.at[kind, n],
                a_recv.at[kind, n],
                section,
                sibling,
            )
            for n, side in enumerate((1 - x, x))
        ]

    def fold_x(kind, cores):
        cores[0].wait_recv()
        crossing = []
        for d in far_first:
            to_x[kind, d] = (
                terms[kind, core, 1 - x, d].astype(F32)
                + from_core[kind, 1 - x, d].astype(F32)
            ).astype(BF16)
            crossing.append((d, push_x(kind, d)))
        to_x[kind, 0] = (
            terms[kind, core, 1 - x, 0].astype(F32)
            + from_core[kind, 1 - x, 0].astype(F32)
        ).astype(BF16)
        crossing.append((0, push_x(kind, 0)))
        cores[1].wait_recv()
        return crossing

    def push_x(kind, d):
        return push(
            to_x.at[kind, d],
            from_x.at[kind, d],
            b_send.at[kind, d],
            b_recv.at[kind, d],
            section,
            across,
        )

    def give_back(kind, crossing):
        returns = []
        for d, copy in crossing:
            copy.wait_recv()
            total = (
                terms[kind, core, x, d].astype(F32)
                + from_core[kind, x, d].astype(F32)
                + from_x[kind, d].astype(F32)
            ).astype(BF16)
            if d == 0:
                returned[kind] = total
                local = pltpu.make_async_copy(
                    returned.at[kind], returned_hbm.at[kind, w], store_sem.at[1 + kind]
                )
                local.start()
                stores.append(local)
            else:
                to_owner[kind, d] = total
                returns.append(
                    push(
                        to_owner.at[kind, d],
                        returned_hbm.at[kind, w],
                        c_send.at[kind, d],
                        c_recv.at[kind, d],
                        section,
                        owner(lax.rem(w + experts - d, experts)),
                    )
                )
        return returns

    loads[0].wait()
    to_wire(wide_a, dot(pick_rows, tokens[...]), slots)
    dispatch(0, wide_a)
    pl.semaphore_wait(barrier, experts + 2)
    send_z(0)
    to_across(0, 0)
    for load in loads[2:5]:
        load.start()
    loads[1].wait()
    cot_rows = dot(pick_rows, cot[...])
    to_wire(wide_b, slot_gate * cot_rows, slots)
    dispatch(1, wide_b)
    send_z(1)
    to_across(1, 0)
    slot_info[:, :width] = cot_rows
    slot_info[:, width : width + tok_count] = pick
    slot_info[:, width + tok_count :] = pick_gate
    slot_store = pltpu.make_async_copy(slot_info, slot_hbm, store_sem.at[0])
    slot_store.start()
    spread(0)
    spread(1)
    pass_on(0)
    loads[2].wait()
    loads[3].wait()
    loads[4].wait()
    collect(0, wide_a, rows_in)
    both_pre = dot(rows_in[...], w_both[...], transposed)
    gate_pre = both_pre[:, :units]
    up_pre = both_pre[:, units:]
    sigmoid = jax.nn.sigmoid(gate_pre)
    activated = gate_pre * sigmoid
    slope = sigmoid * (1.0 + gate_pre * (1.0 - sigmoid))
    hidden = (activated * up_pre).astype(BF16)
    hidden_own[...] = hidden
    pass_on(1)
    product_to_wire(wide_a, hidden, w_down)
    out_cores = fold_cores(0, wide_a)
    mirrored = [push(hidden_own, hidden_other, p_send.at[1], p_recv.at[1], mirror, me)]

    collect(1, wide_b, rows_scaled)
    upper = jnp.where(section >= sections // 2, 1, 0)
    own_cols = pl.ds(pl.multiple_of(upper * half, half), half)
    other_cols = pl.ds(pl.multiple_of((1 - upper) * half, half), half)
    mirrored.append(
        push(
            rows_scaled.at[:, other_cols],
            scaled_other,
            p_send.at[0],
            p_recv.at[0],
            mirror,
            me,
        )
    )
    out_crossing = fold_x(0, out_cores)
    hidden_grad = dot(rows_scaled[...], w_down[...], transposed)
    grad_gate = (hidden_grad * up_pre * slope).astype(BF16)
    grad_up = (hidden_grad * activated).astype(BF16)
    product_to_wire(wide_b, jnp.concatenate([grad_gate, grad_up], axis=1), w_both)
    grad_cores = fold_cores(1, wide_b)
    returns = give_back(0, out_crossing)
    grad_crossing = fold_x(1, grad_cores)
    returns += give_back(1, grad_crossing)
    down_own = dot(hidden_own[...], rows_scaled[:, own_cols], ((0,), (0,)))
    down_own = down_own.astype(BF16)
    for copy in mirrored:
        copy.wait_recv()
    down_other = dot(hidden_other[...], scaled_other[...], ((0,), (0,)))
    down_grad[0] = (
        down_own.astype(F32) + down_other.astype(BF16).astype(F32)
    ).astype(BF16)
    down_store = pltpu.make_async_copy(down_grad, down_grad_hbm, store_sem.at[3])
    down_store.start()
    for store in stores + [slot_store, down_store]:
        store.wait()
    for copy in returns:
        copy.wait_recv()
    for copy in outgoing:
        copy.wait_send()


def combine_kernel(
    experts,
    capacity,
    returned_ref,
    slot_ref,
    ids_ref,
    down_ref,
    mixed_ref,
    token_ref,
    gate_grad_ref,
    down_grad_ref,
    wide_a,
    wide_b,
):
    slots = slot_ref.shape[0]
    tok_count, width = mixed_ref.shape
    pieces = width // LANES
    part = capacity * pieces
    down_grad_ref[...] = down_ref[...]
    for e in range(experts):
        wide_a[e * part : (e + 1) * part] = returned_ref[0, e].astype(F32)
        wide_b[e * part : (e + 1) * part] = returned_ref[1, e].astype(F32)
    if slots > experts * capacity:
        rest = slice(experts * part, slots * pieces)
        zero = jnp.zeros((slots * pieces - experts * part, LANES), F32)
        wide_a[rest] = zero
        wide_b[rest] = zero
    pick = slot_ref[:, width : width + tok_count]
    pick_gate = slot_ref[:, width + tok_count :]
    high = pick_gate.astype(BF16).astype(F32)
    mid = (pick_gate - high).astype(BF16).astype(F32)
    low = pick_gate - high - mid
    terms = jnp.concatenate([low, mid, high], axis=0).T.astype(BF16)
    narrow_pick = pick.T.astype(BF16)
    value = jnp.zeros((slots, LANES), F32)
    span = 4 if pieces % 4 == 0 else 1
    for first in range(0, pieces, span):
        cols = slice(first * LANES, (first + span) * LANES)
        outs = []
        grads = []
        for j in range(first, first + span):
            out = wide_a[pl.ds(j, slots, stride=pieces), :]
            value += slot_ref[:, j * LANES : (j + 1) * LANES] * out
            outs.append(out.astype(BF16))
            grads.append(wide_b[pl.ds(j, slots, stride=pieces), :].astype(BF16))
        out = jnp.concatenate(outs, axis=1)
        mixed_ref[:, cols] = dot(terms, jnp.concatenate([out] * 3, axis=0)).astype(BF16)
        token_ref[:, cols] = dot(narrow_pick, jnp.concatenate(grads, axis=1)).astype(
            BF16
        )
    spread = pick * jnp.sum(value, axis=1, keepdims=True)
    for k, here in enumerate(named_slots(ids_ref[...], slots, experts, capacity)):
        gate_grad_ref[k : k + 1, :] = jnp.sum(
            jnp.where(here, spread, 0.0), axis=0, keepdims=True
        )


def body(sections, devices, tokens, cotangent, expert_ids, gates, w_gate, w_up, w_down):
    tok_count, width = tokens.shape
    capacity = tok_count // 24
    experts = devices // WS
    units = w_gate.shape[2]
    pieces = width // LANES
    part = capacity * pieces
    slots = -(-experts * capacity // 16) * 16
    rows = devices * capacity
    dma = pltpu.SemaphoreType.DMA
    anywhere = pl.BlockSpec(memory_space=pl.ANY)
    vmem = pl.BlockSpec(memory_space=pltpu.VMEM)
    ids_turned = expert_ids.T
    returned, slot_info, down = pl.pallas_call(
        functools.partial(moe_kernel, sections, devices, capacity),
        out_shape=(
            jax.ShapeDtypeStruct((2, experts, part, LANES), BF16),
            jax.ShapeDtypeStruct((slots, width + 2 * tok_count), F32),
            jax.ShapeDtypeStruct((1, units, width // 2), BF16),
        ),
        in_specs=[anywhere] * 7,
        out_specs=(anywhere,) * 3,
        scratch_shapes=[
            pltpu.VMEM(ids_turned.shape, jnp.int32),
            pltpu.VMEM(ids_turned.shape, F32),
            pltpu.VMEM((tok_count, width), BF16),
            pltpu.VMEM((tok_count, width), BF16),
            pltpu.VMEM((2 * units, width), BF16),
            pltpu.VMEM((units, width), BF16),
            pltpu.VMEM((rows * pieces, LANES), F32),
            pltpu.VMEM((rows * pieces, LANES), F32),
            pltpu.VMEM((2, experts, part, LANES), BF16),
            pltpu.VMEM((2, WS, experts, part, LANES), BF16),
            pltpu.VMEM((rows, width), BF16),
            pltpu.VMEM((rows, width), BF16),
            pltpu.VMEM((rows, units), BF16),
            pltpu.VMEM((rows, units), BF16),
            pltpu.VMEM((rows, width // 2), BF16),
            pltpu.VMEM((2, 2, 2, experts, part, LANES), BF16),
            pltpu.VMEM((2, 2, experts, part, LANES), BF16),
            pltpu.VMEM((2, experts, part, LANES), BF16),
            pltpu.VMEM((2, experts, part, LANES), BF16),
            pltpu.VMEM((2, experts, part, LANES), BF16),
            pltpu.VMEM((2, part, LANES), BF16),
            pltpu.VMEM((slots, width + 2 * tok_count), F32),
            pltpu.VMEM((1, units, width // 2), BF16),
            dma((7,)),
            dma((4,)),
            dma((2, experts)),
            dma((2, experts)),
            dma((2, experts)),
            dma((2, experts)),
            dma((2, 2)),
            dma((2, 2)),
            dma((2,)),
            dma((2,)),
            dma((2, 2)),
            dma((2, 2)),
            dma((2, experts)),
            dma((2, experts)),
            dma((2, experts)),
            dma((2, experts)),
        ],
        compiler_params=pltpu.CompilerParams(
            collective_id=0, has_side_effects=True, vmem_limit_bytes=60 << 20
        ),
        cost_estimate=pl.CostEstimate(
            flops=16 * rows * width * units,
            bytes_accessed=6 * width * units + 12 * tok_count * width,
            transcendentals=rows * units,
        ),
    )(
        tokens,
        cotangent,
        ids_turned,
        gates.T,
        jnp.swapaxes(w_gate, 1, 2),
        jnp.swapaxes(w_up, 1, 2),
        w_down,
    )
    mixed_out, token_grad, gate_grad, down_grad = pl.pallas_call(
        functools.partial(combine_kernel, experts, capacity),
        out_shape=(
            jax.ShapeDtypeStruct((tok_count, width), BF16),
            jax.ShapeDtypeStruct((tok_count, width), BF16),
            jax.ShapeDtypeStruct(ids_turned.shape, F32),
            jax.ShapeDtypeStruct((1, units, width // 2), BF16),
        ),
        in_specs=[vmem] * 4,
        out_specs=(vmem,) * 4,
        scratch_shapes=[
            pltpu.VMEM((slots * pieces, LANES), F32),
            pltpu.VMEM((slots * pieces, LANES), F32),
        ],
        compiler_params=pltpu.CompilerParams(vmem_limit_bytes=60 << 20),
        cost_estimate=pl.CostEstimate(
            flops=8 * slots * width * tok_count,
            bytes_accessed=8 * tok_count * width,
            transcendentals=0,
        ),
    )(returned, slot_info, ids_turned, down)
    return mixed_out, token_grad, gate_grad.T, down_grad


def solution(mesh):
    rows = P(("pipe", "expert"), None)
    return jax.shard_map(
        functools.partial(body, mesh.shape["pipe"], mesh.shape["expert"]),
        mesh=mesh,
        in_specs=(
            rows,
            rows,
            rows,
            rows,
            P("pipe", None, "expert"),
            P("pipe", None, "expert"),
            P("pipe", "expert", None),
        ),
        out_specs=(rows, rows, rows, P("pipe", "expert", None)),
        check_vma=False,
    )
```
